128 devices in a mesh: fsdp: 8 (over z, x_lo), cp: 8 (over y, x_hi), tp: 2 (over core).
Axes of the slice: x: 4 (x_hi: 2, x_lo: 2; x = x_hi * 2 + x_lo), y: 4, z: 4, core: 2. Of those that a mesh axis runs over, the one named last changes fastest.
Arguments:
- tokens: bfloat16 [16, 1024, 2048], P('fsdp', 'cp'), may hold values from -6 to 6
- segment_ids: int32 [16, 1024], P('fsdp', 'cp'), may hold values from 0 to 3, as said below
- cotangent: bfloat16 [16, 1024, 2048], P('fsdp', 'cp'), may hold values from -6 to 6
- norm1_gain: bfloat16 [2048], P(('fsdp', 'cp')), may hold values from 0.5 to 1.5
- q_weight: bfloat16 [2048, 2048], P(('fsdp', 'cp'), 'tp'), may hold values from -0.125 to 0.125
- k_weight: bfloat16 [2048, 256], P(('fsdp', 'cp'), 'tp'), may hold values from -0.125 to 0.125
- v_weight: bfloat16 [2048, 256], P(('fsdp', 'cp'), 'tp'), may hold values from -0.125 to 0.125
- o_weight: bfloat16 [2048, 2048], P(('fsdp', 'cp'), 'tp'), may hold values from -0.5 to 0.5
- norm2_gain: bfloat16 [2048], P(('fsdp', 'cp')), may hold values from 0.5 to 1.5
- gate_weight: bfloat16 [2048, 5632], P(('fsdp', 'cp'), 'tp'), may hold values from -0.125 to 0.125
- up_weight: bfloat16 [2048, 5632], P(('fsdp', 'cp'), 'tp'), may hold values from -0.125 to 0.125
- down_weight: bfloat16 [2048, 5632], P(('fsdp', 'cp'), 'tp'), may hold values from -0.078125 to 0.078125
Outputs:
- out: bfloat16 [16, 1024, 2048], P('fsdp', 'cp')
- x_grad: bfloat16 [16, 1024, 2048], P('fsdp', 'cp')
- norm1_gain_grad: float32 [2048], P(('fsdp', 'cp'))
- q_weight_grad: float32 [2048, 2048], P(('fsdp', 'cp'), 'tp')
- k_weight_grad: float32 [2048, 256], P(('fsdp', 'cp'), 'tp')
- v_weight_grad: float32 [2048, 256], P(('fsdp', 'cp'), 'tp')
- o_weight_grad: float32 [2048, 2048], P(('fsdp', 'cp'), 'tp')
- norm2_gain_grad: float32 [2048], P(('fsdp', 'cp'))
- gate_weight_grad: float32 [2048, 5632], P(('fsdp', 'cp'), 'tp')
- up_weight_grad: float32 [2048, 5632], P(('fsdp', 'cp'), 'tp')
- down_weight_grad: float32 [2048, 5632], P(('fsdp', 'cp'), 'tp')
The draws below stay inside these ranges and needn't reach their ends.
Inputs may be any that keep to these rules, and one draw needn't show every extreme that they name: `segment_ids`: taken in the order of true positions pos, each sequence's segment numbers never fall.
All inputs are finite; a program needn't handle non-finite values.
Results may differ from the reference program's by a relative error of at most 0.018.
Values may be sent and summed in bfloat16 or wider, within the bound.
No kernel may reach another device: no remote copies, remote signals or barrier semaphores. Data moves between devices by JAX's collectives and lax.ppermute only.
A program may use at most 384 MiB of HBM per device.

```python
import jax
import jax.numpy as jnp
from jax import lax

D = 2048
HEADS = 32
KV_HEADS = 4
HEAD_DIM = 64
FF = 5632
SEQ_LEN = 1024
KV_DIM = 256
SEQS = 16
SPANS = 16
SPAN = 64


def draw_segment_ids(key, part):
    key = jax.random.fold_in(key, 5)
    keys = jax.random.split(key, 3)
    first_cut = jax.random.randint(keys[0], (SEQS, 1), 1, SPAN)
    middle_cut = jax.random.randint(keys[1], (SEQS, 1), SEQ_LEN // 4, 3 * SEQ_LEN // 4 + 1)
    last_cut = SEQ_LEN - jax.random.randint(keys[2], (SEQS, 1), 1, SPAN)
    places = jnp.arange(SEQ_LEN, dtype=jnp.int32)[None, :]
    natural = (places >= first_cut).astype(jnp.int32) + (places >= middle_cut).astype(jnp.int32) + (places >= last_cut).astype(jnp.int32)
    blocks = jnp.arange(SPANS, dtype=jnp.int32)
    source = jnp.where(blocks % 2 == 0, blocks // 2, SPANS - 1 - blocks // 2)
    natural = natural.reshape(SEQS, SPANS, SPAN)
    return jnp.take(natural, source, axis=1).reshape(SEQS, SEQ_LEN)


def levels(rng, shape, cuts, smallest, largest):
    gain = 1.0
    for axis_at, shards_of in cuts:
        steps = jax.random.uniform(jax.random.fold_in(jax.random.fold_in(rng, 6), axis_at), (shards_of,), jnp.float32, smallest / len(cuts), largest / len(cuts))
        gain = gain * jnp.repeat(jnp.exp(steps), shape[axis_at] // shards_of).reshape((-1,) + (1,) * (len(shape) - 1 - axis_at))
    return gain


def noise(key, shape, scale, limit, shards=(), kind=jnp.bfloat16):
    drawn = jax.random.normal(key, shape, jnp.float32) * scale
    if len(shards) > 0:
        drawn = levels(key, shape, shards, -0.22, 0.18) * drawn
    return jnp.clip(drawn, min=-limit, max=limit).astype(kind)


def setup_inputs(seed: int = 0) -> dict:
    key_list = jax.random.split(jax.random.key(seed), 13)
    tokens = noise(key_list[0], (SEQS, SEQ_LEN, D), 1.0, 6.0, ((0, 8), (1, 8)))
    segment_ids = draw_segment_ids(jax.random.fold_in(key_list[12], 71), 0)
    cotangent = noise(key_list[2], (SEQS, SEQ_LEN, D), 1.0, 6.0, ((0, 8), (1, 8)))
    norm1_gain = jnp.clip(1.0 + 0.1 * jax.random.normal(key_list[3], (D,), jnp.float32), 0.5, 1.5).astype(jnp.bfloat16)
    q_weight = noise(key_list[4], (D, D), D ** -0.5, 0.125, ((0, 64), (1, 2)))
    k_weight = noise(key_list[5], (D, KV_DIM), D ** -0.5, 0.125, ((0, 64), (1, 2)))
    v_weight = noise(key_list[6], (D, KV_DIM), D ** -0.5, 0.125, ((0, 64), (1, 2)))
    o_weight = noise(key_list[7], (D, D), (D // 16) ** -0.5, 0.5, ((0, 64), (1, 2)))
    norm2_gain = jnp.clip(1.0 + 0.1 * jax.random.normal(key_list[8], (D,), jnp.float32), 0.5, 1.5).astype(jnp.bfloat16)
    gate_weight = noise(key_list[9], (D, FF), D ** -0.5, 0.125, ((0, 64), (1, 2)))
    up_weight = noise(key_list[10], (D, FF), D ** -0.5, 0.125, ((0, 64), (1, 2)))
    down_weight = noise(key_list[11], (D, FF), FF ** -0.5, 0.078125, ((0, 64), (1, 2)))
    return dict(tokens=tokens, segment_ids=segment_ids, cotangent=cotangent, norm1_gain=norm1_gain, q_weight=q_weight, k_weight=k_weight, v_weight=v_weight, o_weight=o_weight, norm2_gain=norm2_gain, gate_weight=gate_weight, up_weight=up_weight, down_weight=down_weight)


NORM_EPS = 1e-05
ROPE_BASE = 10000.0
PRECISE = lax.Precision.HIGHEST

@jax.custom_vjp
def low(v):
    return lax.optimization_barrier(v.astype(jnp.bfloat16)).astype(jnp.float32)

@jax.custom_vjp
def low_back(v):
    return v

def low_keep(v):
    return (low(v), None)

def low_pass(kept, grad):
    return (grad,)

def back_keep(v):
    return (v, None)

def back_low(kept, grad):
    return (low(grad),)
low.defvjp(low_keep, low_pass)
low_back.defvjp(back_keep, back_low)

def true_positions(seq_len, block_count):
    block_len = seq_len // block_count
    blocks = jnp.arange(block_count, dtype=jnp.int32)
    source = jnp.where(blocks % 2 == 0, blocks // 2, block_count - 1 - blocks // 2)
    return (source[:, None] * block_len + jnp.arange(block_len, dtype=jnp.int32)[None, :]).reshape(-1)

def angle_tables(positions):
    inverse = ROPE_BASE ** (-jnp.arange(0, HEAD_DIM // 2, dtype=jnp.float32) * 2.0 / HEAD_DIM)
    angles = positions.astype(jnp.float32)[:, None] * inverse[None, :]
    angles = jnp.concatenate([angles, angles], -1)
    return (jnp.cos(angles)[:, None, :], jnp.sin(angles)[:, None, :])

def rotate(values, cosines, sines):
    half_dim = values.shape[-1] // 2
    turned = jnp.concatenate([-values[..., half_dim:], values[..., :half_dim]], -1)
    return values * cosines + turned * sines

def block_layer(tokens, segments, gain_one, w_query, w_key, w_value, w_output, gain_two, w_gate, w_up, w_down):
    seq_len = tokens.shape[0]
    positions = true_positions(seq_len, SPANS)
    cosines, sines = angle_tables(positions)
    inv_one = lax.rsqrt(lax.optimization_barrier(jnp.mean(tokens * tokens, -1, keepdims=True)) + NORM_EPS)
    normed = low(tokens * inv_one * gain_one)
    q_pre = low_back(jnp.dot(normed, w_query, precision=PRECISE))
    k_pre = low_back(jnp.dot(normed, w_key, precision=PRECISE))
    v_pre = low_back(jnp.dot(normed, w_value, precision=PRECISE))
    queries = low(rotate(q_pre.reshape(seq_len, HEADS, HEAD_DIM), cosines, sines))
    keys_rot = low(rotate(k_pre.reshape(seq_len, KV_HEADS, HEAD_DIM), cosines, sines))
    values_all = low(v_pre).reshape(seq_len, KV_HEADS, HEAD_DIM)
    group_size = HEADS // KV_HEADS
    block_count = max(1, seq_len // 512)
    block_len = seq_len // block_count
    score_scale = HEAD_DIM ** (-0.5)
    query_blocks = queries.reshape(block_count, block_len, KV_HEADS, group_size, HEAD_DIM)
    position_blocks = positions.reshape(block_count, block_len)
    segment_blocks = segments.reshape(block_count, block_len)

    def attend(pieces):
        query_block, position_block, segment_block = pieces
        scores = low_back(jnp.einsum('rkgd,tkd->kgrt', query_block, keys_rot, precision=PRECISE) * score_scale)
        allowed = (segment_block[:, None] == segments[None, :]) & (positions[None, :] <= position_block[:, None])
        scores = jnp.where(allowed, scores, -jnp.inf)
        probs_low = low(jax.nn.softmax(scores, axis=-1))
        return jnp.einsum('kgrt,tkd->rkgd', probs_low, values_all, precision=PRECISE)
    mixed_heads = lax.map(jax.checkpoint(attend), (query_blocks, position_blocks, segment_blocks))
    attended = low(low_back(mixed_heads.reshape(seq_len, HEADS * HEAD_DIM)))
    middle = tokens + low_back(jnp.dot(attended, w_output.T, precision=PRECISE))
    inv_two = lax.rsqrt(lax.optimization_barrier(jnp.mean(middle * middle, -1, keepdims=True)) + NORM_EPS)
    normed_two = low(middle * inv_two * gain_two)
    gate_pre = low_back(jnp.dot(normed_two, w_gate, precision=PRECISE))
    up_pre = low_back(jnp.dot(normed_two, w_up, precision=PRECISE))
    hidden = low(jax.nn.silu(gate_pre) * up_pre)
    return middle + low_back(jnp.dot(hidden, w_down.T, precision=PRECISE))

def reference(tokens, segment_ids, cotangent, norm1_gain, q_weight, k_weight, v_weight, o_weight, norm2_gain, gate_weight, up_weight, down_weight):
    weights = tuple((weight.astype(jnp.float32) for weight in (norm1_gain, q_weight, k_weight, v_weight, o_weight, norm2_gain, gate_weight, up_weight, down_weight)))

    def one_sequence(totals, pieces):
        seq_tokens, seq_ids, seq_cot = pieces

        def forward(seq_in, gain_one, w_query, w_key, w_value, w_output, gain_two, w_gate, w_up, w_down):
            return block_layer(seq_in, seq_ids, gain_one, w_query, w_key, w_value, w_output, gain_two, w_gate, w_up, w_down)
        outputs, pull_back = jax.vjp(forward, seq_tokens.astype(jnp.float32), *weights)
        grads = pull_back(seq_cot.astype(jnp.float32))
        totals = tuple((total + grad for total, grad in zip(totals, grads[1:])))
        return (totals, (outputs.astype(jnp.bfloat16), grads[0].astype(jnp.bfloat16)))
    zero_grads = tuple((jnp.zeros_like(weight) for weight in weights))
    totals, (outputs, input_grads) = lax.scan(one_sequence, zero_grads, (tokens, segment_ids, cotangent))
    return (outputs, input_grads, totals[0], totals[1], totals[2], totals[3], totals[4], totals[5], totals[6], totals[7], totals[8])
```

```python
import jax
import jax.numpy as jnp
from jax import lax
from jax.experimental import pallas as pl
from jax.experimental.pallas import tpu as pltpu
from jax.sharding import Mesh
from jax.sharding import PartitionSpec as P

HEAD_DIM = 64
NORM_EPS = 1e-05
ROPE_BASE = 10000.0
X_RING = ("xl", "xh")
OFFSETS = (0, -1, 1, 2)
bf16 = jnp.bfloat16
f32 = jnp.float32


def x_index(x):
    return (x % 2) * 2 + x // 2


def shift(v, ring, d):
    if ring == X_RING:
        return lax.ppermute(v, X_RING, [(x_index(i), x_index((i + d) % 4)) for i in range(4)])
    n = 2 if ring in ("c", "xh") else 4
    return lax.ppermute(v, ring, [(i, (i + d) % n) for i in range(n)])


def ring_gather(v, ring):
    half = v.shape[0] // 2
    left = shift(v, ring, 1)
    right = shift(v, ring, -1)
    far_a = shift(left[:half], ring, 1)
    far_b = shift(right[half:], ring, -1)
    return v, left, right, jnp.concatenate([far_a, far_b], 0)


def ring_scatter(own, left, right, far, ring):
    half = far.shape[0] // 2
    a = shift(far[:half], ring, 1)
    b = shift(far[half:], ring, -1)
    up = jnp.concatenate([(right[:half].astype(f32) + a.astype(f32)).astype(bf16), right[half:]], 0)
    down = jnp.concatenate([left[:half], (left[half:].astype(f32) + b.astype(f32)).astype(bf16)], 0)
    u = shift(up, ring, 1)
    d = shift(down, ring, -1)
    return own.astype(f32) + u.astype(f32) + d.astype(f32)


def gather_rows(block, first):
    z = lax.axis_index("z")
    xl = lax.axis_index("xl")
    xh = lax.axis_index("xh")
    x = xh * 2 + xl
    n = block.shape[-1]
    out = jnp.zeros((4, 2, 4, 2, 32, n), block.dtype)
    if first == "z":
        mid = jnp.zeros((4, 4, 32, n), block.dtype)
        for off, part in zip(OFFSETS, ring_gather(block, "z")):
            mid = lax.dynamic_update_slice(mid, part[None], ((z + off) % 4, 0, 0, 0))
        for off, part in zip(OFFSETS, ring_gather(mid, X_RING)):
            xj = (x + off) % 4
            out = lax.dynamic_update_slice(
                out, part[:, None, :, None], (0, xj % 2, 0, xj // 2, 0, 0)
            )
    else:
        mid = jnp.zeros((2, 4, 2, 32, n), block.dtype)
        for off, part in zip(OFFSETS, ring_gather(block, X_RING)):
            xj = (x + off) % 4
            mid = lax.dynamic_update_slice(
                mid, part[None, :, None], (xj % 2, 0, xj // 2, 0, 0)
            )
        for off, part in zip(OFFSETS, ring_gather(mid, "z")):
            out = lax.dynamic_update_slice(out, part[None], ((z + off) % 4, 0, 0, 0, 0, 0))
    return out.reshape(2048, n)


def scatter_rows(grad, first):
    z = lax.axis_index("z")
    xl = lax.axis_index("xl")
    xh = lax.axis_index("xh")
    x = xh * 2 + xl
    n = grad.shape[-1]
    g = grad.reshape(4, 2, 4, 2, 32, n)
    if first == "x":
        parts = []
        for off in OFFSETS:
            xj = (x + off) % 4
            parts.append(
                lax.dynamic_slice(g, (0, xj % 2, 0, xj // 2, 0, 0), (4, 1, 4, 1, 32, n)).reshape(4, 4, 32, n)
            )
        g = ring_scatter(*parts, X_RING).astype(bf16)
        parts = [lax.dynamic_index_in_dim(g, (z + off) % 4, 0, False) for off in OFFSETS]
        return ring_scatter(*parts, "z").astype(bf16)
    parts = [lax.dynamic_index_in_dim(g, (z + off) % 4, 0, False) for off in OFFSETS]
    g = ring_scatter(*parts, "z").astype(bf16)
    parts = []
    for off in OFFSETS:
        xj = (x + off) % 4
        parts.append(lax.dynamic_slice(g, (xj % 2, 0, xj // 2, 0, 0), (1, 4, 1, 32, n)).reshape(4, 32, n))
    return ring_scatter(*parts, X_RING).astype(bf16)


def positions_of(y, xh):
    rows = []
    o = jnp.arange(64, dtype=jnp.int32)
    for off in OFFSETS:
        i = ((y + off) % 4) * 2 + xh
        rows += [i * 64 + o, (15 - i) * 64 + o]
    return jnp.concatenate(rows)


def rope_tables(positions, heads):
    inverse = ROPE_BASE ** (-jnp.arange(0, HEAD_DIM // 2, dtype=f32) * 2.0 / HEAD_DIM)
    angles = positions.astype(f32)[:, None] * inverse[None, :]
    cos = jnp.cos(angles)
    sin = jnp.sin(angles)
    cos = jnp.tile(jnp.concatenate([cos, cos], -1), (1, heads))
    sin = jnp.tile(jnp.concatenate([-sin, sin], -1), (1, heads))
    return cos, sin


def swap_halves(u):
    lane = lax.broadcasted_iota(jnp.int32, u.shape, 1)
    return jnp.where(lane % HEAD_DIM < HEAD_DIM // 2, jnp.roll(u, -32, 1), jnp.roll(u, 32, 1))


def rotate(u, cos, sin):
    w = u.shape[1]
    return u * cos[:, :w] + swap_halves(u) * sin[:, :w]


def rotate_back(w, cos, sin):
    n = w.shape[1]
    return w * cos[:, :n] + swap_halves(w * sin[:, :n])


def dot(a, b):
    return jnp.dot(a, b, preferred_element_type=f32)


def dot_nt(a, b):
    return lax.dot_general(a, b, (((1,), (1,)), ((), ())), preferred_element_type=f32)


def dot_tn(a, b):
    return lax.dot_general(a, b, (((0,), (0,)), ((), ())), preferred_element_type=f32)


def mask_of(qpos, qseg, kpos, kseg):
    return jnp.where((qseg == kseg) & (kpos <= qpos), 0.0, -jnp.inf).astype(f32)


def attend_kernel(q_ref, kv_ref, kv2_ref, qpos_ref, qseg_ref, kpos_ref, kseg_ref, out_ref, log_ref):
    mask = mask_of(qpos_ref[...], qseg_ref[...], kpos_ref[...], kseg_ref[...])
    outs, logs = [], []
    for g in range(2):
        keys = jnp.concatenate([kv_ref[:, g * 64 : g * 64 + 64], kv2_ref[:, g * 64 : g * 64 + 64]], 0)
        values = jnp.concatenate(
            [kv_ref[:, 128 + g * 64 : 192 + g * 64], kv2_ref[:, 128 + g * 64 : 192 + g * 64]], 0
        )
        for h in range(4):
            at = (g * 4 + h) * 64
            s = dot_nt(q_ref[:, at : at + 64] * jnp.asarray(0.125, bf16), keys) + mask
            top = jnp.max(s, -1, keepdims=True)
            p = jnp.exp(s - top)
            total = jnp.sum(p, -1, keepdims=True)
            outs.append(dot(p.astype(bf16), values) / total)
            logs.append(top + jnp.log(total))
    out_ref[...] = jnp.concatenate(outs, 1).astype(bf16)
    log_ref[...] = jnp.concatenate(logs, 1)


def attend(q, kv, kv2, qpos, qseg, kpos, kseg):
    tile = 128
    rows = q.shape[0]
    whole = lambda a: pl.BlockSpec(a.shape, lambda i: (0, 0))
    tiled = lambda a: pl.BlockSpec((tile, a.shape[1]), lambda i: (i, 0))
    return pl.pallas_call(
        attend_kernel,
        grid=(rows // tile,),
        in_specs=[tiled(q), whole(kv), whole(kv2), tiled(qpos), tiled(qseg), whole(kpos), whole(kseg)],
        out_specs=[tiled(q), pl.BlockSpec((tile, 8), lambda i: (i, 0))],
        out_shape=[
            jax.ShapeDtypeStruct(q.shape, bf16),
            jax.ShapeDtypeStruct((rows, 8), f32),
        ],
        compiler_params=pltpu.CompilerParams(vmem_limit_bytes=40 << 20),
        cost_estimate=pl.CostEstimate(flops=2 << 30, bytes_accessed=2 << 20, transcendentals=4 << 20),
        name="attend",
    )(q, kv, kv2, qpos, qseg, kpos, kseg)


def attend_back_kernel(
    q_ref, g_ref, log_ref, kv_ref, kv2_ref, qpos_ref, qseg_ref, kpos_ref, kseg_ref, dq_ref, dkv_ref, dkv2_ref
):
    @pl.when(pl.program_id(0) == 0)
    def _():
        dkv_ref[...] = jnp.zeros_like(dkv_ref)
        dkv2_ref[...] = jnp.zeros_like(dkv2_ref)

    mask = mask_of(qpos_ref[...], qseg_ref[...], kpos_ref[...], kseg_ref[...])
    half = kv_ref.shape[0]
    for g in range(2):
        keys = jnp.concatenate([kv_ref[:, g * 64 : g * 64 + 64], kv2_ref[:, g * 64 : g * 64 + 64]], 0)
        values = jnp.concatenate(
            [kv_ref[:, 128 + g * 64 : 192 + g * 64], kv2_ref[:, 128 + g * 64 : 192 + g * 64]], 0
        )
        dk = jnp.zeros((2 * half, 64), f32)
        dv = jnp.zeros((2 * half, 64), f32)
        for h in range(4):
            at = (g * 4 + h) * 64
            q = q_ref[:, at : at + 64] * jnp.asarray(0.125, bf16)
            grad = g_ref[:, at : at + 64]
            s = dot_nt(q, keys) + mask
            p = jnp.exp(s - log_ref[:, g * 4 + h : g * 4 + h + 1])
            dp = dot_nt(grad, values)
            t = p * dp
            ds = (t - p * jnp.sum(t, -1, keepdims=True)).astype(bf16)
            dq_ref[:, at : at + 64] = dot(ds, keys) * 0.125
            dk += dot_tn(ds, q)
            dv += dot_tn(p.astype(bf16), grad)
        dkv_ref[:, g * 64 : g * 64 + 64] += dk[:half]
        dkv2_ref[:, g * 64 : g * 64 + 64] += dk[half:]
        dkv_ref[:, 128 + g * 64 : 192 + g * 64] += dv[:half]
        dkv2_ref[:, 128 + g * 64 : 192 + g * 64] += dv[half:]


def attend_back(q, grad, logs, kv, kv2, qpos, qseg, kpos, kseg):
    tile = 128
    rows = q.shape[0]
    whole = lambda a: pl.BlockSpec(a.shape, lambda i: (0, 0))
    tiled = lambda a: pl.BlockSpec((tile, a.shape[1]), lambda i: (i, 0))
    return pl.pallas_call(
        attend_back_kernel,
        grid=(rows // tile,),
        in_specs=[
            tiled(q),
            tiled(grad),
            tiled(logs),
            whole(kv),
            whole(kv2),
            tiled(qpos),
            tiled(qseg),
            whole(kpos),
            whole(kseg),
        ],
        out_specs=[tiled(q), whole(kv), whole(kv)],
        out_shape=[
            jax.ShapeDtypeStruct(q.shape, f32),
            jax.ShapeDtypeStruct(kv.shape, f32),
            jax.ShapeDtypeStruct(kv.shape, f32),
        ],
        compiler_params=pltpu.CompilerParams(vmem_limit_bytes=48 << 20),
        cost_estimate=pl.CostEstimate(flops=5 << 30, bytes_accessed=4 << 20, transcendentals=4 << 20),
        name="attend_back",
    )(q, grad, logs, kv, kv2, qpos, qseg, kpos, kseg)


def inverse_rms(v):
    return lax.rsqrt(jnp.mean(v * v, -1, keepdims=True) + NORM_EPS)


def norm_back(grad_normed, inputs, inv_rms, gain):
    scaled = grad_normed * gain
    return inv_rms * scaled - inputs * inv_rms**3 * jnp.mean(scaled * inputs, -1, keepdims=True)


def blocks(v):
    return tuple(v[k * 128 : (k + 1) * 128] for k in range(4))


def layer(
    tokens,
    segment_ids,
    cotangent,
    norm1_gain,
    q_weight,
    k_weight,
    v_weight,
    o_weight,
    norm2_gain,
    gate_weight,
    up_weight,
    down_weight,
):
    y = lax.axis_index("y")
    xh = lax.axis_index("xh")
    core = lax.axis_index("c")
    own = lambda a: lax.dynamic_index_in_dim(a, core, 0, False)
    x_own = own(tokens)
    ct_own = own(cotangent)

    gains = lax.all_gather(
        jnp.stack([norm1_gain, norm2_gain], 0), ("z", "xl", "y", "xh"), axis=1, tiled=True
    ).astype(f32)

    def per_chip(*arrays):
        joined = jnp.concatenate([a.reshape(32, 4, -1) for a in arrays], -1)
        return lax.all_to_all(joined.transpose(1, 0, 2), "y", 0, 0, tiled=True)

    twice = lambda a: jnp.repeat(a.reshape(32, 2, 64), 2, axis=1)
    attn_block = per_chip(q_weight, twice(k_weight), twice(v_weight), o_weight)
    x_all = jnp.concatenate(ring_gather(x_own, "y"), 0)
    seg_all = jnp.concatenate(ring_gather(own(segment_ids)[:, None], "y"), 0)
    w_qkv = gather_rows(attn_block[:, :, :384], "z")
    w_o = gather_rows(attn_block[:, :, 384:], "x")
    w_qkv2 = shift(w_qkv, "c", 1)
    w_o2 = shift(w_o, "c", 1)

    gu_block = per_chip(gate_weight, up_weight)
    down_block = per_chip(down_weight)
    ct_all = jnp.concatenate(ring_gather(ct_own, "y"), 0)
    w_gu = gather_rows(gu_block, "z")
    w_down = gather_rows(down_block, "x")
    w_gu2 = shift(w_gu, "c", 1)
    w_down2 = shift(w_down, "c", 1)

    qpos = positions_of(y, xh)
    kpos = jnp.concatenate([qpos, positions_of(y, 1 - xh)])
    cos, sin = rope_tables(qpos, 4)
    x_f = x_all.astype(f32)
    inv_one = inverse_rms(x_f)
    h1 = (x_f * inv_one * gains[0]).astype(bf16)

    def project(w):
        pre = dot(h1, w)
        return (
            rotate(pre[:, :256], cos, sin).astype(bf16),
            rotate(pre[:, 256:320], cos, sin).astype(bf16),
            pre[:, 320:].astype(bf16),
        )

    q_a, k_a, v_a = project(w_qkv)
    q_b, k_b, v_b = project(w_qkv2)
    queries = jnp.concatenate([q_a, q_b], 1)
    kv = jnp.concatenate([k_a, k_b, v_a, v_b], 1)
    kv2 = shift(kv, "xh", 1)
    seg2 = shift(seg_all, "xh", 1)
    qp = qpos[:, None]
    kp = kpos[None, :]
    kseg = jnp.concatenate([seg_all, seg2], 0).reshape(1, -1)
    attended, logs = attend(queries, kv, kv2, qp, seg_all, kp, kseg)
    o_part = (dot_nt(attended[:, :256], w_o) + dot_nt(attended[:, 256:], w_o2)).astype(bf16)
    middle = x_own.astype(f32) + ring_scatter(*blocks(o_part), "y")

    inv_two = inverse_rms(middle)
    h2_own = (middle * inv_two * gains[1]).astype(bf16)
    h2 = jnp.concatenate(ring_gather(h2_own, "y"), 0)

    def hidden_of(w_gu_s, w_down_s):
        pre = dot(h2, w_gu_s)
        gate, up = pre[:, :704], pre[:, 704:]
        sig = jax.nn.sigmoid(gate)
        hidden = (gate * sig * up).astype(bf16)
        d_hidden = dot(ct_all, w_down_s)
        d_gate = (d_hidden * up * sig * (1.0 + gate * (1.0 - sig))).astype(bf16)
        d_up = (d_hidden * gate * sig).astype(bf16)
        return hidden, jnp.concatenate([d_gate, d_up], 1)

    hid_a, d_gu_a = hidden_of(w_gu, w_down)
    hid_b, d_gu_b = hidden_of(w_gu2, w_down2)
    d_h2_part = (dot_nt(d_gu_a, w_gu) + dot_nt(d_gu_b, w_gu2)).astype(bf16)
    out_part = (dot_nt(hid_a, w_down) + dot_nt(hid_b, w_down2)).astype(bf16)
    d_h2 = ring_scatter(*blocks(d_h2_part), "y")
    g_down = dot_tn(ct_all, hid_a) + shift(dot_tn(ct_all, hid_b).astype(bf16), "c", 1).astype(f32)
    g_gu = dot_tn(h2, d_gu_a) + shift(dot_tn(h2, d_gu_b).astype(bf16), "c", 1).astype(f32)
    gain_two_grad = jnp.sum(d_h2 * middle * inv_two, 0)
    d_middle = ct_own.astype(f32) + norm_back(d_h2, middle, inv_two, gains[1])
    da_own = d_middle.astype(bf16)
    da = jnp.concatenate(ring_gather(da_own, "y"), 0)
    out_own = (middle + ring_scatter(*blocks(out_part), "y")).astype(bf16)

    g_o = dot_tn(da, attended[:, :256]) + shift(
        dot_tn(da, attended[:, 256:]).astype(bf16), "c", 1
    ).astype(f32)
    d_att = jnp.concatenate([dot(da, w_o), dot(da, w_o2)], 1).astype(bf16)
    d_q, d_kv, d_kv2 = attend_back(queries, d_att, logs, kv, kv2, qp, seg_all, kp, kseg)
    d_kv = d_kv + shift(d_kv2.astype(bf16), "xh", 1).astype(f32)
    dq_a = rotate_back(d_q[:, :256], cos, sin)
    dq_b = rotate_back(d_q[:, 256:], cos, sin)
    dk = rotate_back(d_kv[:, :128], cos, sin)
    d_a = jnp.concatenate([dq_a, dk[:, :64], d_kv[:, 128:192]], 1).astype(bf16)
    d_b = jnp.concatenate([dq_b, dk[:, 64:], d_kv[:, 192:]], 1).astype(bf16)
    d_h1_full = dot_nt(d_a, w_qkv) + dot_nt(d_b, w_qkv2)
    gain_one_grad = jnp.sum(d_h1_full * x_f * inv_one, 0)
    d_h1 = ring_scatter(*blocks(d_h1_full.astype(bf16)), "y")
    g_qkv = dot_tn(h1, d_a) + shift(dot_tn(h1, d_b).astype(bf16), "c", 1).astype(f32)
    dx_own = (d_middle + norm_back(d_h1, x_own.astype(f32), inv_one[:128], gains[0])).astype(bf16)

    def to_owner(grad, first):
        part = scatter_rows(grad.astype(bf16), first)
        got = lax.all_to_all(part, "y", 0, 0, tiled=True)
        return got.astype(f32)

    def columns(got):
        return got.transpose(1, 0, 2).reshape(32, -1)

    own_down = to_owner(g_down, "z")
    own_gu = to_owner(g_gu, "x")
    own_o = to_owner(g_o, "z")
    own_qkv = to_owner(g_qkv, "x")
    gain_grads = jnp.stack([gain_one_grad, gain_two_grad], 0).reshape(2, 64, 32).transpose(1, 0, 2)
    gain_got = lax.all_to_all(gain_grads, ("z", "xl", "y", "xh"), 0, 0, tiled=True).sum(0)
    gain_got = gain_got + shift(gain_got, "c", 1)

    pair = lambda a: a.reshape(2, 2, 32, 64).sum(1).transpose(1, 0, 2).reshape(32, 128)

    def both(a):
        other = shift(a, "c", 1)
        return jnp.where(core == 0, jnp.stack([a, other]), jnp.stack([other, a]))

    return (
        both(out_own),
        both(dx_own),
        gain_got[0],
        columns(own_qkv[:, :, :256]),
        pair(own_qkv[:, :, 256:320]),
        pair(own_qkv[:, :, 320:]),
        columns(own_o),
        gain_got[1],
        columns(own_gu[:, :, :704]),
        columns(own_gu[:, :, 704:]),
        columns(own_down),
    )


def solution(mesh):
    fine = Mesh(mesh.devices.reshape(4, 2, 4, 2, 2), ("z", "xl", "y", "xh", "c"))
    fsdp, cp = ("z", "xl"), ("y", "xh")
    acts, gain, weight = P(fsdp, cp, None), P(fsdp + cp), P(fsdp + cp, "c")
    return jax.shard_map(
        layer,
        mesh=fine,
        in_specs=(acts, P(fsdp, cp), acts, gain, weight, weight, weight, weight, gain, weight, weight, weight),
        out_specs=(acts, acts, gain, weight, weight, weight, weight, gain, weight, weight, weight),
        check_vma=False,
    )
```

```python
import jax
import jax.numpy as jnp
from jax import lax
from jax.experimental import pallas as pl
from jax.experimental.pallas import tpu as pltpu
from jax.sharding import Mesh
from jax.sharding import PartitionSpec as P

HEAD_DIM = 64
NORM_EPS = 1e-05
ROPE_BASE = 10000.0
X_RING = ("xl", "xh")
OFFSETS = (0, -1, 1, 2)
LIGHT = pl.CostEstimate(flops=1 << 20, bytes_accessed=1 << 16, transcendentals=0)
bf16 = jnp.bfloat16
f32 = jnp.float32


def x_index(x):
    return (x % 2) * 2 + x // 2


def shift(v, ring, d):
    if ring == X_RING:
        return lax.ppermute(v, X_RING, [(x_index(i), x_index((i + d) % 4)) for i in range(4)])
    n = 2 if ring in ("c", "xh") else 4
    return lax.ppermute(v, ring, [(i, (i + d) % n) for i in range(n)])


def gather_near(v, ring):
    return shift(v, ring, 1), shift(v, ring, -1)


def gather_far(near, ring):
    left, right = near
    half = left.shape[0] // 2
    return shift(left[:half], ring, 1), shift(right[half:], ring, -1)


def gathered(v, near, far):
    return jnp.concatenate([v, *near, *far], 0)


def sum_far(parts, ring):
    return shift(parts[3], ring, 1), shift(parts[4], ring, -1)


def sum_pass(parts, far):
    half = parts[3].shape[0]
    left, right = parts[1], parts[2]
    up = jnp.concatenate([(right[:half].astype(f32) + far[0].astype(f32)).astype(bf16), right[half:]], 0)
    down = jnp.concatenate([left[:half], (left[half:].astype(f32) + far[1].astype(f32)).astype(bf16)], 0)
    return up, down


def sum_near(passed, ring):
    return shift(passed[0], ring, 1), shift(passed[1], ring, -1)


def sum_of(parts, near):
    return parts[0].astype(f32) + near[0].astype(f32) + near[1].astype(f32)


def together(*values):
    return lax.optimization_barrier(values)


TORUS = ("z", "xh", "xl")


def gather_torus(block):
    n = block.shape[-1]
    return lax.all_gather(block.reshape(128, n), TORUS, axis=0, tiled=True)


def positions_of(y, xh):
    rows = []
    o = jnp.arange(64, dtype=jnp.int32)
    for off in OFFSETS:
        i = ((y + off) % 4) * 2 + xh
        rows += [i * 64 + o, (15 - i) * 64 + o]
    return jnp.concatenate(rows)


def rope_tables(positions):
    inverse = ROPE_BASE ** (-jnp.arange(0, HEAD_DIM // 2, dtype=f32) * 2.0 / HEAD_DIM)
    angles = positions.astype(f32)[:, None] * inverse[None, :]
    cos = jnp.cos(angles)
    sin = jnp.sin(angles)
    return jnp.concatenate([cos] * 4, -1), jnp.concatenate([-sin, sin] * 2, -1)


def swap_halves(u):
    lane = lax.broadcasted_iota(jnp.int32, u.shape, 1)
    return jnp.where(lane % HEAD_DIM < HEAD_DIM // 2, pltpu.roll(u, u.shape[1] - 32, 1), pltpu.roll(u, 32, 1))


def wide(table, width):
    return jnp.concatenate([table] * (width // 128), 1)


def rotate(u, cos, sin):
    w = u.shape[1]
    return u * wide(cos, w) + swap_halves(u) * wide(sin, w)


def rotate_back(w, cos, sin):
    n = w.shape[1]
    return w * wide(cos, n) + swap_halves(w * wide(sin, n))


def dot(a, b):
    return jnp.dot(a, b, preferred_element_type=f32)


def dot_nt(a, b):
    return lax.dot_general(a, b, (((1,), (1,)), ((), ())), preferred_element_type=f32)


def dot_tn(a, b):
    return lax.dot_general(a, b, (((0,), (0,)), ((), ())), preferred_element_type=f32)


ROWS = (128, 128, 128, 64, 64)
STARTS = (0, 128, 256, 384, 448)
Q_LANES = pl.BlockSpec((4, 2, 2, 4, 32, 256), lambda *_: (0,) * 6)
O_LANES = pl.BlockSpec((4, 2, 2, 4, 32, 256), lambda *_: (0, 0, 0, 0, 0, 1))
KV_LANES = pl.BlockSpec((4, 2, 2, 4, 32, 128), lambda *_: (0, 0, 0, 0, 0, 4))
NOTE_LANES = pl.BlockSpec((4, 2, 2, 4, 32, 128), lambda *_: (0, 0, 0, 0, 0, 5))
MASKED = -1e30
PIECES = [pl.BlockSpec((r, 2048), lambda *_: (0, 0)) for r in ROWS]
PIECE_SHAPES = [jax.ShapeDtypeStruct((r, 2048), bf16) for r in ROWS]


def whole(*shape):
    return pl.BlockSpec(shape, lambda *_: (0,) * len(shape))


def in_order(ref, slot_ref, z, lanes):
    return jnp.concatenate(
        [ref[z, xh, xl, slot_ref[y], :, lanes] for xl in range(2) for y in range(4) for xh in range(2)], 0
    )


def weight_of(ref, slot_ref):
    return jnp.concatenate([in_order(ref, slot_ref, z, slice(None)) for z in range(4)], 0)


def project_kv_kernel(slot_ref, *refs):
    pieces, refs = refs[:5], refs[5:]
    note_ref, wa_ref, wb_ref, cos_ref, sin_ref, h1_ref, inv_ref, kv_ref, gain_ref, seg_ref = refs
    notes = lambda at: jnp.concatenate(
        [
            note_ref[z, xh, xl, slot_ref[y], 0:1, at : at + 32]
            for z in range(4)
            for xl in range(2)
            for y in range(4)
            for xh in range(2)
        ],
        1,
    ).astype(f32)
    gain_ref[0:1] = notes(0)
    gain_ref[1:2] = notes(32)
    z, xl, xh = slot_ref[4], slot_ref[5], slot_ref[6]
    for k in range(2):
        row = [note_ref[z, (xh + k) % 2, xl, j, 1:2, :] for j in range(4)]
        seg_ref[k : k + 1] = jnp.concatenate(row, 1).astype(f32)
    for ref, start, rows in zip(pieces, STARTS, ROWS):
        x = ref[...].astype(f32)
        inv = lax.rsqrt(jnp.mean(x * x, -1, keepdims=True) + NORM_EPS)
        inv_ref[start : start + rows] = inv
        h1_ref[start : start + rows] = (x * inv * gain_ref[0:1]).astype(bf16)
    a = dot(h1_ref[...], weight_of(wa_ref, slot_ref))
    b = dot(h1_ref[...], weight_of(wb_ref, slot_ref))
    keys = rotate(jnp.concatenate([a[:, :64], b[:, :64]], 1), cos_ref[...], sin_ref[...])
    kv_ref[...] = jnp.concatenate([keys[:, :64], a[:, 64:], keys[:, 64:], b[:, 64:]], 1).astype(bf16)


def with_slots(grid, in_specs, out_specs, scratch=(), mib=16):
    return dict(
        grid_spec=pltpu.PrefetchScalarGridSpec(
            num_scalar_prefetch=1, grid=(grid,), in_specs=in_specs, out_specs=out_specs, scratch_shapes=scratch
        ),
        compiler_params=pltpu.CompilerParams(vmem_limit_bytes=mib << 20),
        cost_estimate=LIGHT,
    )


def project_kv(slots, pieces, w, w2, cos, sin):
    return pl.pallas_call(
        project_kv_kernel,
        out_shape=[
            jax.ShapeDtypeStruct((512, 2048), bf16),
            jax.ShapeDtypeStruct((512, 1), f32),
            jax.ShapeDtypeStruct((512, 256), bf16),
            jax.ShapeDtypeStruct((2, 2048), f32),
            jax.ShapeDtypeStruct((2, 512), f32),
        ],
        name="project_kv",
        **with_slots(
            1,
            PIECES + [NOTE_LANES, KV_LANES, KV_LANES, whole(512, 128), whole(512, 128)],
            [whole(512, 2048), whole(512, 1), whole(512, 256), whole(2, 2048), whole(2, 512)],
            mib=56,
        ),
    )(slots, *pieces, w, w, w2, cos, sin)


def project_q_kernel(slot_ref, h1_ref, wa_ref, wb_ref, cos_ref, sin_ref, q_ref):
    for k, w_ref in enumerate((wa_ref, wb_ref)):
        q = rotate(dot(h1_ref[...], weight_of(w_ref, slot_ref)), cos_ref[...], sin_ref[...])
        q_ref[:, k * 256 : (k + 1) * 256] = q.astype(bf16)


def project_q(slots, h1, w, w2, cos, sin):
    rows = lambda n: pl.BlockSpec((256, n), lambda i, _: (i, 0))
    return pl.pallas_call(
        project_q_kernel,
        out_shape=jax.ShapeDtypeStruct((512, 512), bf16),
        name="project_q",
        **with_slots(2, [rows(2048), Q_LANES, Q_LANES, rows(128), rows(128)], rows(512), mib=56),
    )(slots, h1, w, w2, cos, sin)


def set_mask(mask_ref, qpos_ref, qseg_ref, kpos_ref, kseg_ref):
    @pl.when(pl.program_id(0) == 0)
    def _():
        column = lambda ref: jnp.concatenate([jnp.broadcast_to(ref[...], (128, 512)).T] * 4, 1)
        allowed = (column(kseg_ref) == qseg_ref[...]) & (column(kpos_ref) <= qpos_ref[...])
        mask_ref[...] = jnp.where(allowed, 0.0, MASKED)


def attend_kernel(last, slot_ref, q_ref, kv_ref, qpos_ref, qseg_ref, kpos_ref, kseg_ref, *refs):
    mask_ref = refs[-1]
    set_mask(mask_ref, qpos_ref, qseg_ref, kpos_ref, kseg_ref)
    before, stats_before, out_ref, stats_ref = refs[:4] if last else (None, None, *refs[:2])
    turned = kv_ref[...].T
    outs = []
    for h in range(2):
        q = q_ref[:, h * 64 : h * 64 + 64] * jnp.asarray(0.125, bf16)
        s = dot_nt(kv_ref[:, :64], q) + mask_ref[...]
        top = jnp.max(s, 0, keepdims=True)
        p = jnp.exp(s - top)
        total = jnp.sum(p, 0, keepdims=True)
        out = dot(turned[64:], p.astype(bf16))
        if last:
            top_1, total_1 = stats_before[0, h : h + 1], stats_before[0, 2 + h : 3 + h]
            peak = jnp.maximum(top, top_1)
            scale_1, scale = jnp.exp(top_1 - peak), jnp.exp(top - peak)
            total = scale_1 * total_1 + scale * total
            out = (scale_1 * before[h * 64 : h * 64 + 64] + scale * out) / total
            stats_ref[0, h : h + 1] = peak + jnp.log(total)
        else:
            stats_ref[0, h : h + 1] = top
            stats_ref[0, 2 + h : 3 + h] = total
        outs.append(out)
    out = jnp.concatenate(outs, 0)
    out_ref[...] = out.T.astype(bf16) if last else out


LANES = pl.BlockSpec((512, 128), lambda i, _: (0, i))
GROUP = pl.BlockSpec((512, 128), lambda i, _: (0, i // 2))
TURNED = pl.BlockSpec((128, 512), lambda i, _: (i, 0))
STATS = pl.BlockSpec((1, 8, 512), lambda i, _: (i, 0, 0))


def attend(slots, q, kv, places, before=()):
    last = len(before) > 0
    return pl.pallas_call(
        lambda *refs: attend_kernel(last, *refs),
        out_shape=[
            jax.ShapeDtypeStruct((512, 512), bf16 if last else f32),
            jax.ShapeDtypeStruct((4, 8, 512), f32),
        ],
        name="attend",
        **with_slots(
            4,
            [LANES, GROUP] + [whole(1, 512)] * 4 + [TURNED, STATS] * last,
            [LANES if last else TURNED, STATS],
            [pltpu.VMEM((512, 512), f32)],
        ),
    )(slots, q, kv, *places, *before)


def o_part_kernel(slot_ref, att_ref, wa_ref, wb_ref, *parts):
    for z in range(4):
        lanes = slice(z * 512, (z + 1) * 512)
        o_a = in_order(wa_ref, slot_ref, z, slice(None))
        o_b = in_order(wb_ref, slot_ref, z, slice(None))
        total = dot_nt(att_ref[:, :256], o_a) + dot_nt(att_ref[:, 256:], o_b)
        for ref, start, rows in zip(parts, STARTS, ROWS):
            ref[:, lanes] = total[start : start + rows].astype(bf16)


def o_part_of(slots, attended, w, w2):
    return pl.pallas_call(
        o_part_kernel,
        out_shape=PIECE_SHAPES,
        name="o_part_of",
        **with_slots(1, [whole(512, 512), O_LANES, O_LANES], PIECES),
    )(slots, attended, w, w2)


def d_att_kernel(slot_ref, *refs):
    pieces, (wa_ref, wb_ref, da_ref, d_att_ref) = refs[:5], refs[5:]
    for ref, start, rows in zip(pieces, STARTS, ROWS):
        da_ref[start : start + rows] = ref[...]
    d_att_ref[:, :256] = dot(da_ref[...], weight_of(wa_ref, slot_ref)).astype(bf16)
    d_att_ref[:, 256:] = dot(da_ref[...], weight_of(wb_ref, slot_ref)).astype(bf16)


def d_att_of(slots, pieces, w, w2):
    return pl.pallas_call(
        d_att_kernel,
        out_shape=[jax.ShapeDtypeStruct((512, 2048), bf16), jax.ShapeDtypeStruct((512, 512), bf16)],
        name="d_att_of",
        **with_slots(1, PIECES + [O_LANES, O_LANES], [whole(512, 2048), whole(512, 512)], mib=56),
    )(slots, *pieces, w, w2)


def attend_back_kernel(last, slot_ref, q_ref, kv_ref, qpos_ref, qseg_ref, kpos_ref, kseg_ref, *refs):
    g_ref, att_ref, stats_ref, *refs = refs
    before, cos_ref, sin_ref, dq_ref, dkv_ref = refs[:5] if last else (None, None, None, *refs[:2])
    mask_ref, sum_ref = refs[-2:]
    set_mask(mask_ref, qpos_ref, qseg_ref, kpos_ref, kseg_ref)
    turned = kv_ref[...].T
    inner = (g_ref[...].astype(f32) * att_ref[...].astype(f32)).T
    dqs = []
    dk = jnp.zeros((512, 64), f32)
    dv = jnp.zeros((512, 64), f32)
    for h in range(2):
        lanes = slice(h * 64, h * 64 + 64)
        q = q_ref[:, lanes] * jnp.asarray(0.125, bf16)
        g = g_ref[:, lanes]
        p = jnp.exp(dot_nt(kv_ref[:, :64], q) + mask_ref[...] - stats_ref[0, h : h + 1])
        dp = dot_nt(kv_ref[:, 64:], g)
        ds = (p * (dp - jnp.sum(inner[lanes], 0, keepdims=True))).astype(bf16)
        dk += dot(ds, q)
        dv += dot(p.astype(bf16), g)
        dqs.append(dot(turned[:64], ds))
    new = jnp.concatenate([dk, dv], 1)

    @pl.when(pl.program_id(0) % 2 == 0)
    def _():
        sum_ref[...] = new

    @pl.when(pl.program_id(0) % 2 == 1)
    def _():
        sum_ref[...] += new

    dkv_ref[...] = sum_ref[...].astype(dkv_ref.dtype)
    dq = jnp.concatenate(dqs, 0)
    if last:
        dq = ((dq + before[...]) * 0.125).T
        dq_ref[...] = rotate_back(dq, cos_ref[...], sin_ref[...]).astype(bf16)
    else:
        dq_ref[...] = dq


def attend_back(slots, q, kv, places, g, attended, stats, before=(), tables=()):
    last = len(tables) > 0
    return pl.pallas_call(
        lambda *refs: attend_back_kernel(last, *refs),
        out_shape=[
            jax.ShapeDtypeStruct((512, 512), bf16 if last else f32),
            jax.ShapeDtypeStruct((512, 256), f32 if last else bf16),
        ],
        name="attend_back",
        **with_slots(
            4,
            [LANES, GROUP]
            + [whole(1, 512)] * 4
            + [LANES, LANES, STATS]
            + [TURNED, whole(512, 128), whole(512, 128)] * last,
            [LANES if last else TURNED, GROUP],
            [pltpu.VMEM((512, 512), f32), pltpu.VMEM((512, 128), f32)],
        ),
    )(slots, q, kv, *places, g, attended, stats, *before, *tables)


def d_h1_kernel(slot_ref, dq_ref, dkv_ref, dkv2_ref, cos_ref, sin_ref, qa_ref, qb_ref, kva_ref, kvb_ref, *refs):
    pieces, inv_ref, (da_ref, db_ref, gain_ref), parts = refs[:5], refs[5], refs[6:9], refs[9:]
    d_kv = dkv_ref[...] + dkv2_ref[...].astype(f32)
    dk = rotate_back(jnp.concatenate([d_kv[:, :64], d_kv[:, 128:192]], 1), cos_ref[...], sin_ref[...])
    da_ref[...] = jnp.concatenate([dk[:, :64], d_kv[:, 64:128]], 1).astype(bf16)
    db_ref[...] = jnp.concatenate([dk[:, 64:], d_kv[:, 192:]], 1).astype(bf16)
    for z in range(4):
        lanes = slice(z * 512, (z + 1) * 512)
        total = (
            dot_nt(dq_ref[:, :256], in_order(qa_ref, slot_ref, z, slice(None)))
            + dot_nt(dq_ref[:, 256:], in_order(qb_ref, slot_ref, z, slice(None)))
            + dot_nt(da_ref[...], in_order(kva_ref, slot_ref, z, slice(None)))
            + dot_nt(db_ref[...], in_order(kvb_ref, slot_ref, z, slice(None)))
        )
        gain = jnp.zeros((1, 512), f32)
        for ref, part, start, rows in zip(pieces, parts, STARTS, ROWS):
            mine = total[start : start + rows]
            part[:, lanes] = mine.astype(bf16)
            scaled = ref[:, lanes].astype(f32) * inv_ref[start : start + rows]
            gain += jnp.sum(mine * scaled, 0, keepdims=True)
        for k in range(16):
            gain_ref[z * 16 + k : z * 16 + k + 1] = gain[:, k * 32 : k * 32 + 32]


def d_h1_of(slots, dq, d_kv, d_kv2, cos, sin, w, w2, x_pieces, inv):
    return pl.pallas_call(
        d_h1_kernel,
        out_shape=[
            jax.ShapeDtypeStruct((512, 128), bf16),
            jax.ShapeDtypeStruct((512, 128), bf16),
            jax.ShapeDtypeStruct((64, 32), f32),
        ]
        + PIECE_SHAPES,
        name="d_h1_of",
        **with_slots(
            1,
            [whole(512, 512), whole(512, 256), whole(512, 256), whole(512, 128), whole(512, 128)]
            + [Q_LANES, Q_LANES, KV_LANES, KV_LANES]
            + PIECES
            + [whole(512, 1)],
            [whole(512, 128), whole(512, 128), whole(64, 32)] + PIECES,
            mib=28,
        ),
    )(slots, dq, d_kv, d_kv2, cos, sin, w, w2, w, w2, *x_pieces, inv)


def inverse_rms(v):
    return lax.rsqrt(jnp.mean(v * v, -1, keepdims=True) + NORM_EPS)


def norm_back(grad_normed, inputs, inv_rms, gain):
    scaled = grad_normed * gain
    return inv_rms * scaled - inputs * inv_rms**3 * jnp.mean(scaled * inputs, -1, keepdims=True)


UNITS = 768
PARTS = 3 * UNITS


def hidden_kernel(slot_ref, *refs):
    pieces, ct_ref, refs, h2_ref = refs[:5], refs[5], refs[6:], refs[18]

    @pl.when(pl.program_id(0) == 0)
    def _():
        for ref, start, rows in zip(pieces, STARTS, ROWS):
            h2_ref[start : start + rows] = ref[...]

    for s in range(2):
        gate_ref, up_ref, down_ref = refs[3 * s : 3 * s + 3]
        hid_ref, dg_ref, du_ref = refs[6 + 3 * s : 9 + 3 * s]
        gate = dot(h2_ref[...], weight_of(gate_ref, slot_ref))
        up = dot(h2_ref[...], weight_of(up_ref, slot_ref))
        d_hidden = dot(ct_ref[...], weight_of(down_ref, slot_ref))
        sig = jax.nn.sigmoid(gate)
        act = gate * sig
        hid_ref[...] = (act * up).astype(bf16)
        dg_ref[...] = (d_hidden * up * sig * (1.0 + gate * (1.0 - sig))).astype(bf16)
        du_ref[...] = (d_hidden * act).astype(bf16)


def hidden_of(slots, h2, ct, rows, rows2):
    tile = 256
    steps = UNITS // tile
    part = lambda p: pl.BlockSpec((4, 2, 2, 4, 32, tile), lambda i, _: (0, 0, 0, 0, 0, p * steps + i))
    out = pl.BlockSpec((512, tile), lambda i, _: (0, i))
    view = lambda r: r.reshape(4, 2, 2, 4, 32, PARTS)
    return pl.pallas_call(
        hidden_kernel,
        grid_spec=pltpu.PrefetchScalarGridSpec(
            num_scalar_prefetch=1,
            grid=(steps,),
            in_specs=PIECES + [whole(512, 2048)] + [part(p) for p in range(3)] * 2,
            out_specs=[out] * 6 + [whole(512, 2048)],
        ),
        out_shape=[jax.ShapeDtypeStruct((512, UNITS), bf16)] * 6 + [jax.ShapeDtypeStruct((512, 2048), bf16)],
        compiler_params=pltpu.CompilerParams(vmem_limit_bytes=56 << 20),
        cost_estimate=LIGHT,
        name="hidden_of",
    )(slots, *h2, ct, *([view(rows)] * 3), *([view(rows2)] * 3))


def back_kernel(count, slot_ref, *refs):
    acts, weights, outs = refs[: 2 * count], refs[2 * count : 2 * count + 2], refs[2 * count + 2 :]
    total = None
    for s in range(2):
        for k in range(count):
            lanes = slice(k * UNITS, (k + 1) * UNITS)
            term = dot_nt(acts[s * count + k][...], in_order(weights[s], slot_ref, 0, lanes))
            total = term if total is None else total + term
    for ref, start, rows in zip(outs, STARTS, ROWS):
        ref[...] = total[start : start + rows].astype(bf16)


def back_through(slots, acts, rows, rows2, first):
    count = len(acts) // 2
    acts_spec = pl.BlockSpec((512, UNITS), lambda z, _: (0, 0))
    weight = pl.BlockSpec((1, 2, 2, 4, 32, count * UNITS), lambda z, _: (z, 0, 0, 0, 0, first // count))
    view = lambda r: r.reshape(4, 2, 2, 4, 32, PARTS)
    return pl.pallas_call(
        lambda *refs: back_kernel(count, *refs),
        grid_spec=pltpu.PrefetchScalarGridSpec(
            num_scalar_prefetch=1,
            grid=(4,),
            in_specs=[acts_spec] * (2 * count) + [weight] * 2,
            out_specs=[pl.BlockSpec((r, 512), lambda z, _: (0, z)) for r in ROWS],
        ),
        out_shape=[jax.ShapeDtypeStruct((r, 2048), bf16) for r in ROWS],
        compiler_params=pltpu.CompilerParams(vmem_limit_bytes=(56 if count > 1 else 22) << 20),
        cost_estimate=LIGHT,
        name="back_through",
    )(slots, *acts, view(rows), view(rows2))


def grad_kernel(lefts, widths, extras, slot_ref, *refs):
    out_ref = refs[-1]
    left_refs, rights = refs[: max(lefts) + 1], refs[max(lefts) + 1 :]
    other_ref = rights[len(lefts)] if "other" in extras else None
    turned = [ref[...].T for ref in left_refs]
    start = 0
    for k, width in enumerate(widths):
        lanes = slice(start, start + width)
        grad = dot(turned[lefts[k]], rights[k][...])
        at = 0
        for xl in range(2):
            for y in range(4):
                for xh in range(2):
                    rows = grad[at : at + 32]
                    if other_ref is not None:
                        rows = rows + other_ref[0, xh, xl, slot_ref[y], :, lanes].astype(f32)
                    out_ref[0, xh, xl, slot_ref[y], :, lanes] = rows.astype(bf16)
                    at += 32
        start += width
    if "notes" in extras:
        note_refs = rights[-3:-1]
        first = lax.broadcasted_iota(jnp.int32, (32, 128), 0) == 0
        at = 0
        for xl in range(2):
            for y in range(4):
                for xh in range(2):
                    row = jnp.concatenate([ref[at : at + 1] for ref in note_refs] + [jnp.zeros((1, 64), f32)], 1)
                    rows = jnp.where(first, jnp.broadcast_to(row, (32, 128)), 0.0)
                    out_ref[0, xh, xl, slot_ref[y], :, start : start + 128] = rows.astype(bf16)
                    at += 1


def weight_grads(slots, left, rights, other=None, notes=None):
    widths = [width for _, _, _, width in rights]
    total = sum(widths) + (128 if notes is not None else 0)
    features = pl.BlockSpec((512, 512), lambda z, _: (0, z))
    block = pl.BlockSpec((1, 2, 2, 4, 32, total), lambda z, _: (z, 0, 0, 0, 0, 0))
    lane_block = lambda at, width: pl.BlockSpec((512, width), lambda z, _: (0, at // width))
    specs = [features] * len(left) + [lane_block(at, width) for _, _, at, width in rights]
    args = list(left) + [a for _, a, _, _ in rights]
    extras = []
    if other is not None:
        extras.append("other")
        specs.append(pl.BlockSpec((1, 2, 2, 4, 32, sum(widths)), lambda z, _: (z, 0, 0, 0, 0, 0)))
        args.append(other)
    if notes is not None:
        extras.append("notes")
        specs += [pl.BlockSpec((16, 32), lambda z, _: (z, 0))] * 2
        args += list(notes)
    lefts = [k for k, _, _, _ in rights]
    return pl.pallas_call(
        lambda *refs: grad_kernel(lefts, widths, extras, *refs),
        out_shape=jax.ShapeDtypeStruct((4, 2, 2, 4, 32, total), bf16),
        name="weight_grads",
        **with_slots(4, specs, block, mib=56 if total == PARTS else 28),
    )(slots, *args)


def layer(
    tokens,
    segment_ids,
    cotangent,
    norm1_gain,
    q_weight,
    k_weight,
    v_weight,
    o_weight,
    norm2_gain,
    gate_weight,
    up_weight,
    down_weight,
):
    y = lax.axis_index("y")
    xh = lax.axis_index("xh")
    core = lax.axis_index("c")
    own = lambda a: lax.dynamic_index_in_dim(a, core, 0, False)
    x_own = own(tokens)
    ct_own = own(cotangent)
    qpos = positions_of(y, xh)
    cos, sin = rope_tables(qpos)
    qpos = qpos.astype(f32)[None]
    far_pos = positions_of(y, 1 - xh).astype(f32)[None]
    x_near = gather_near(x_own, "y")

    split = lambda a: a.reshape(32, 4, -1)
    padded = lambda a: jnp.pad(split(a), ((0, 0), (0, 0), (0, UNITS - 704)))
    twice = lambda a: jnp.repeat(a.reshape(32, 2, 64), 2, axis=1)
    notes = jnp.concatenate([norm1_gain, norm2_gain, jnp.zeros((64,), bf16)])
    notes = jnp.stack([notes, own(segment_ids).astype(bf16)], 0)
    notes = jnp.broadcast_to(jnp.pad(notes, ((0, 30), (0, 0)))[:, None], (32, 4, 128))
    attn = jnp.concatenate(
        [split(q_weight), split(o_weight), twice(k_weight), twice(v_weight), notes], -1
    ).transpose(1, 0, 2)
    mlp = jnp.concatenate([padded(gate_weight), padded(up_weight), padded(down_weight)], -1).transpose(1, 0, 2)

    def by_slot(block):
        pick = lambda d: lax.dynamic_index_in_dim(block, (y + d) % 4, 0, False)
        return jnp.stack([pick(0)] + [shift(pick(-off), "y", -off) for off in OFFSETS[1:]], 0)

    slots = jnp.array((0, 2, 3, 1), jnp.int32)[(jnp.arange(4, dtype=jnp.int32) - y) % 4]
    slots = jnp.concatenate([slots, jnp.stack([lax.axis_index("z"), lax.axis_index("xl"), xh])])
    to_torus = lambda a: lax.all_to_all(a, TORUS, 0, 0, tiled=True)
    six = lambda a: a.reshape(4, 2, 2, 4, 32, -1)
    attn = by_slot(attn).reshape(1, 128, 768)
    attn, mlp, cos, sin, slots, qpos, far_pos = together(attn, mlp, cos, sin, slots, qpos, far_pos)
    mlp = by_slot(mlp)
    w_attn = to_torus(jnp.broadcast_to(attn, (16, 128, 768)))
    x_far = gather_far(x_near, "y")
    ct_near = gather_near(ct_own, "y")
    x_far, ct_near = together(x_far, ct_near)
    w_attn, mlp, x_far, ct_near = together(w_attn, mlp, x_far, ct_near)
    mlp_rows = gather_torus(mlp)
    w_attn2 = six(shift(w_attn, "c", 1))
    w_attn = six(w_attn)

    x_pieces = (x_own, *x_near, *x_far)
    h1, inv_one, kv, gains, ids = project_kv(slots, x_pieces, w_attn, w_attn2, cos, sin)
    h1, kv = together(h1, kv)
    kv2 = shift(kv, "xh", 1)
    queries = project_q(slots, h1, w_attn, w_attn2, cos, sin)
    own_places = (qpos, ids[:1], qpos, ids[:1])
    far_places = (qpos, ids[:1], far_pos, ids[1:])
    first = attend(slots, queries, kv, own_places)
    first, kv2 = together(first, kv2)
    attended, stats = attend(slots, queries, kv2, far_places, first)
    o_part = o_part_of(slots, attended, w_attn, w_attn2)
    o_far = sum_far(o_part, "y")
    o_pass = sum_pass(o_part, o_far)
    o_near = sum_near(o_pass, "y")
    o_pass, ct_near = together(o_pass, ct_near)
    ct_far = gather_far(ct_near, "y")
    ct_all = gathered(ct_own, ct_near, ct_far)
    o_near, ct_all = together(o_near, ct_all)
    middle = x_own.astype(f32) + sum_of(o_part, o_near)

    inv_two = inverse_rms(middle)
    h2_own = (middle * inv_two * gains[1]).astype(bf16)
    h2_near = gather_near(h2_own, "y")
    mlp_rows, h2_own = together(mlp_rows, h2_own)
    mlp_rows2 = shift(mlp_rows, "c", 1)
    h2_pieces = (h2_own, *h2_near, *gather_far(h2_near, "y"))
    hid_a, dg_a, du_a, hid_b, dg_b, du_b, h2 = hidden_of(slots, h2_pieces, ct_all, mlp_rows, mlp_rows2)
    d_h2_part = back_through(slots, (dg_a, du_a, dg_b, du_b), mlp_rows, mlp_rows2, 0)

    def mlp_grads(h2, hid, dg, du, other=None):
        rights = [(0, dg, 0, UNITS), (0, du, 0, UNITS), (1, hid, 0, UNITS)]
        return weight_grads(slots, (h2, ct_all), rights, other)

    d_h2_part, h2 = together(d_h2_part, h2)
    d_h2_far = sum_far(d_h2_part, "y")
    grads_b = mlp_grads(h2, hid_b, dg_b, du_b)
    d_h2_far, grads_b = together(d_h2_far, grads_b)
    grads_b2 = shift(grads_b, "c", 1)
    d_h2_pass = sum_pass(d_h2_part, d_h2_far)
    d_h2_pass, hid_a = together(d_h2_pass, hid_a)
    d_h2_near = sum_near(d_h2_pass, "y")
    out_part = back_through(slots, (hid_a, hid_b), mlp_rows, mlp_rows2, 2)
    d_h2_near, out_part = together(d_h2_near, out_part)
    d_h2 = sum_of(d_h2_part, d_h2_near)
    gain_two_grad = jnp.sum(d_h2 * middle * inv_two, 0).reshape(64, 32)
    d_middle = ct_own.astype(f32) + norm_back(d_h2, middle, inv_two, gains[1])
    da_own = d_middle.astype(bf16)
    da_own, h2 = together(da_own, h2)
    da_near = gather_near(da_own, "y")
    mlp_grad = mlp_grads(h2, hid_a, dg_a, du_a, grads_b2)
    da_near, mlp_grad, gain_two_grad = together(da_near, mlp_grad, gain_two_grad)
    da_far = gather_far(da_near, "y")
    da_pieces = (da_own, *da_near, *da_far)

    da, d_att = d_att_of(slots, da_pieces, w_attn, w_attn2)
    out_part, d_att = together(out_part, d_att)
    out_far = sum_far(out_part, "y")
    dq_far, d_kv2 = attend_back(slots, queries, kv2, far_places, d_att, attended, stats)
    d_kv2 = shift(d_kv2, "xh", 1)
    dq, d_kv = attend_back(
        slots, queries, kv, own_places, d_att, attended, stats, (dq_far,), (cos, sin)
    )
    dq, d_kv, d_kv2, out_far = together(dq, d_kv, d_kv2, out_far)
    dkv_a, dkv_b, gain_one_grad, *d_h1_part = d_h1_of(
        slots, dq, d_kv, d_kv2, cos, sin, w_attn, w_attn2, x_pieces, inv_one
    )
    d_h1_part, h1 = together(d_h1_part, h1)
    d_h1_far = sum_far(d_h1_part, "y")
    def attn_grads(h1, at, dkv, other=None, notes=None):
        rights = [(0, dq, at, 256), (1, attended, at, 256), (0, dkv, 0, 128)]
        return weight_grads(slots, (h1, da), rights, other, notes)

    grads_2 = attn_grads(h1, 256, dkv_b)
    d_h1_far, grads_2, out_far = together(d_h1_far, grads_2, out_far)
    grads_2 = shift(grads_2, "c", 1)
    d_h1_near = sum_near(sum_pass(d_h1_part, d_h1_far), "y")
    out_near = sum_near(sum_pass(out_part, out_far), "y")
    grads_1 = attn_grads(h1, 0, dkv_a, grads_2, (gain_one_grad, gain_two_grad))
    mlp_own = lax.psum_scatter(mlp_grad.reshape(2048, PARTS), TORUS, scatter_dimension=0, tiled=True)
    mlp_own, grads_1, d_h1_near, out_near = together(mlp_own, grads_1, d_h1_near, out_near)
    got = to_torus(grads_1.reshape(16, 128, 768))
    def to_y(grads):
        ring = [shift(grads[1], "y", -1), shift(grads[3], "y", 2), shift(grads[2], "y", 1), grads[0]]
        ring = jnp.stack(ring + ring[:3], 0)
        return lax.dynamic_slice_in_dim(ring, 3 - y, 4, 0).astype(f32)

    columns = lambda got: got.transpose(1, 0, 2).reshape(32, -1)
    grads = to_y(mlp_own.reshape(4, 32, PARTS))
    own_gate, own_up, own_down = (columns(grads[:, :, p * UNITS : p * UNITS + 704]) for p in range(3))
    d_h1 = sum_of(d_h1_part, d_h1_near)
    dx_own = (d_middle + norm_back(d_h1, x_own.astype(f32), inv_one[:128], gains[0])).astype(bf16)
    out_own = (middle + sum_of(out_part, out_near)).astype(bf16)

    def both(a):
        other = shift(a, "c", 1)
        return jnp.where(core == 0, jnp.stack([a, other]), jnp.stack([other, a]))

    out, dx = both(out_own), both(dx_own)
    got, own_gate, own_up, own_down, out, dx = together(got, own_gate, own_up, own_down, out, dx)
    grads = to_y(got.astype(f32).sum(0).astype(bf16).reshape(4, 32, 768))
    own_q, own_o, own_kv = grads[:, :, :256], grads[:, :, 256:512], grads[:, :, 512:640]
    gain_got = grads[:, 0, 640:704].sum(0).reshape(2, 32)
    gain_got = gain_got + shift(gain_got, "c", 1)

    pair = lambda a: a.reshape(2, 2, 32, 64).sum(1).transpose(1, 0, 2).reshape(32, 128)

    return (
        out,
        dx,
        gain_got[0],
        columns(own_q),
        pair(own_kv[:, :, :64]),
        pair(own_kv[:, :, 64:]),
        columns(own_o),
        gain_got[1],
        own_gate,
        own_up,
        own_down,
    )


def solution(mesh):
    fine = Mesh(mesh.devices.reshape(4, 2, 4, 2, 2), ("z", "xl", "y", "xh", "c"))
    fsdp, cp = ("z", "xl"), ("y", "xh")
    acts, gain, weight = P(fsdp, cp, None), P(fsdp + cp), P(fsdp + cp, "c")
    return jax.shard_map(
        layer,
        mesh=fine,
        in_specs=(acts, P(fsdp, cp), acts, gain, weight, weight, weight, weight, gain, weight, weight, weight),
        out_specs=(acts, acts, gain, weight, weight, weight, weight, gain, weight, weight, weight),
        check_vma=False,
    )
```

```python
import jax
import jax.numpy as jnp
from jax import lax
from jax.experimental import pallas as pl
from jax.experimental.pallas import tpu as pltpu
from jax.sharding import Mesh
from jax.sharding import PartitionSpec as P

HEAD_DIM = 64
NORM_EPS = 1e-05
ROPE_BASE = 10000.0
X_RING = ("xl", "xh")
OFFSETS = (0, -1, 1, 2)
LIGHT = pl.CostEstimate(flops=1 << 20, bytes_accessed=1 << 16, transcendentals=0)
bf16 = jnp.bfloat16
f32 = jnp.float32


def x_index(x):
    return (x % 2) * 2 + x // 2


def shift(v, ring, d):
    if ring == X_RING:
        return lax.ppermute(v, X_RING, [(x_index(i), x_index((i + d) % 4)) for i in range(4)])
    n = 2 if ring in ("c", "xh") else 4
    return lax.ppermute(v, ring, [(i, (i + d) % n) for i in range(n)])


def gather_near(v, ring):
    return shift(v, ring, 1), shift(v, ring, -1)


def gather_far(near, ring):
    left, right = near
    half = left.shape[0] // 2
    return shift(left[:half], ring, 1), shift(right[half:], ring, -1)


def gathered(v, near, far):
    return jnp.concatenate([v, *near, *far], 0)


def sum_far(parts, ring):
    return shift(parts[3], ring, 1), shift(parts[4], ring, -1)


def sum_pass(parts, far):
    half = parts[3].shape[0]
    left, right = parts[1], parts[2]
    up = jnp.concatenate([(right[:half].astype(f32) + far[0].astype(f32)).astype(bf16), right[half:]], 0)
    down = jnp.concatenate([left[:half], (left[half:].astype(f32) + far[1].astype(f32)).astype(bf16)], 0)
    return up, down


def sum_near(passed, ring):
    return shift(passed[0], ring, 1), shift(passed[1], ring, -1)


def sum_of(parts, near):
    return parts[0].astype(f32) + near[0].astype(f32) + near[1].astype(f32)


def together(*values):
    return lax.optimization_barrier(values)


TORUS = ("z", "xh", "xl")


def gather_torus(block):
    n = block.shape[-1]
    return lax.all_gather(block.reshape(128, n), TORUS, axis=0, tiled=True)


def positions_of(y, xh):
    rows = []
    o = jnp.arange(64, dtype=jnp.int32)
    for off in OFFSETS:
        i = ((y + off) % 4) * 2 + xh
        rows += [i * 64 + o, (15 - i) * 64 + o]
    return jnp.concatenate(rows)


def rope_tables(positions):
    inverse = ROPE_BASE ** (-jnp.arange(0, HEAD_DIM // 2, dtype=f32) * 2.0 / HEAD_DIM)
    angles = positions.astype(f32)[:, None] * inverse[None, :]
    cos = jnp.cos(angles)
    sin = jnp.sin(angles)
    return jnp.concatenate([cos] * 4, -1), jnp.concatenate([-sin, sin] * 2, -1)


def swap_halves(u):
    lane = lax.broadcasted_iota(jnp.int32, u.shape, 1)
    return jnp.where(lane % HEAD_DIM < HEAD_DIM // 2, pltpu.roll(u, u.shape[1] - 32, 1), pltpu.roll(u, 32, 1))


def wide(table, width):
    return jnp.concatenate([table] * (width // 128), 1)


def rotate(u, cos, sin):
    w = u.shape[1]
    return u * wide(cos, w) + swap_halves(u) * wide(sin, w)


def rotate_back(w, cos, sin):
    n = w.shape[1]
    return w * wide(cos, n) + swap_halves(w * wide(sin, n))


def dot(a, b):
    return jnp.dot(a, b, preferred_element_type=f32)


def dot_nt(a, b):
    return lax.dot_general(a, b, (((1,), (1,)), ((), ())), preferred_element_type=f32)


def dot_tn(a, b):
    return lax.dot_general(a, b, (((0,), (0,)), ((), ())), preferred_element_type=f32)


ROWS = (128, 128, 128, 64, 64)
STARTS = (0, 128, 256, 384, 448)
Q_LANES = pl.BlockSpec((4, 2, 2, 4, 32, 256), lambda *_: (0,) * 6)
O_LANES = pl.BlockSpec((4, 2, 2, 4, 32, 256), lambda *_: (0, 0, 0, 0, 0, 1))
KV_LANES = pl.BlockSpec((4, 2, 2, 4, 32, 128), lambda *_: (0, 0, 0, 0, 0, 4))
NOTE_LANES = pl.BlockSpec((4, 2, 2, 4, 32, 128), lambda *_: (0, 0, 0, 0, 0, 5))
MASKED = -1e30
PIECES = [pl.BlockSpec((r, 2048), lambda *_: (0, 0)) for r in ROWS]
PIECE_SHAPES = [jax.ShapeDtypeStruct((r, 2048), bf16) for r in ROWS]


def whole(*shape):
    return pl.BlockSpec(shape, lambda *_: (0,) * len(shape))


def in_order(ref, slot_ref, z, lanes):
    return jnp.concatenate(
        [ref[z, xh, xl, slot_ref[y], :, lanes] for xl in range(2) for y in range(4) for xh in range(2)], 0
    )


def weight_of(ref, slot_ref):
    return jnp.concatenate([in_order(ref, slot_ref, z, slice(None)) for z in range(4)], 0)


def project_kv_kernel(slot_ref, *refs):
    pieces, refs = refs[:5], refs[5:]
    note_ref, wa_ref, wb_ref, cos_ref, sin_ref, h1_ref, inv_ref, kv_ref, gain_ref, seg_ref = refs
    notes = lambda at: jnp.concatenate(
        [
            note_ref[z, xh, xl, slot_ref[y], 0:1, at : at + 32]
            for z in range(4)
            for xl in range(2)
            for y in range(4)
            for xh in range(2)
        ],
        1,
    ).astype(f32)
    gain_ref[0:1] = notes(0)
    gain_ref[1:2] = notes(32)
    z, xl, xh = slot_ref[4], slot_ref[5], slot_ref[6]
    for k in range(2):
        row = [note_ref[z, (xh + k) % 2, xl, j, 1:2, :] for j in range(4)]
        seg_ref[k : k + 1] = jnp.concatenate(row, 1).astype(f32)
    for ref, start, rows in zip(pieces, STARTS, ROWS):
        x = ref[...].astype(f32)
        inv = lax.rsqrt(jnp.mean(x * x, -1, keepdims=True) + NORM_EPS)
        inv_ref[start : start + rows] = inv
        h1_ref[start : start + rows] = (x * inv * gain_ref[0:1]).astype(bf16)
    a = dot(h1_ref[...], weight_of(wa_ref, slot_ref))
    b = dot(h1_ref[...], weight_of(wb_ref, slot_ref))
    keys = rotate(jnp.concatenate([a[:, :64], b[:, :64]], 1), cos_ref[...], sin_ref[...])
    kv_ref[...] = jnp.concatenate([keys[:, :64], a[:, 64:], keys[:, 64:], b[:, 64:]], 1).astype(bf16)


def with_slots(grid, in_specs, out_specs, scratch=(), mib=16):
    return dict(
        grid_spec=pltpu.PrefetchScalarGridSpec(
            num_scalar_prefetch=1, grid=(grid,), in_specs=in_specs, out_specs=out_specs, scratch_shapes=scratch
        ),
        compiler_params=pltpu.CompilerParams(vmem_limit_bytes=mib << 20),
        cost_estimate=LIGHT,
    )


def project_kv(slots, pieces, w, w2, cos, sin):
    return pl.pallas_call(
        project_kv_kernel,
        out_shape=[
            jax.ShapeDtypeStruct((512, 2048), bf16),
            jax.ShapeDtypeStruct((512, 1), f32),
            jax.ShapeDtypeStruct((512, 256), bf16),
            jax.ShapeDtypeStruct((2, 2048), f32),
            jax.ShapeDtypeStruct((2, 512), f32),
        ],
        name="project_kv",
        **with_slots(
            1,
            PIECES + [NOTE_LANES, KV_LANES, KV_LANES, whole(512, 128), whole(512, 128)],
            [whole(512, 2048), whole(512, 1), whole(512, 256), whole(2, 2048), whole(2, 512)],
            mib=56,
        ),
    )(slots, *pieces, w, w, w2, cos, sin)


def project_q_kernel(slot_ref, h1_ref, wa_ref, wb_ref, cos_ref, sin_ref, q_ref):
    for k, w_ref in enumerate((wa_ref, wb_ref)):
        q = rotate(dot(h1_ref[...], weight_of(w_ref, slot_ref)), cos_ref[...], sin_ref[...])
        q_ref[:, k * 256 : (k + 1) * 256] = q.astype(bf16)


def project_q(slots, h1, w, w2, cos, sin):
    rows = lambda n: pl.BlockSpec((256, n), lambda i, _: (i, 0))
    return pl.pallas_call(
        project_q_kernel,
        out_shape=jax.ShapeDtypeStruct((512, 512), bf16),
        name="project_q",
        **with_slots(2, [rows(2048), Q_LANES, Q_LANES, rows(128), rows(128)], rows(512), mib=56),
    )(slots, h1, w, w2, cos, sin)


def set_mask(mask_ref, qpos_ref, qseg_ref, kpos_ref, kseg_ref):
    @pl.when(pl.program_id(0) == 0)
    def _():
        column = lambda ref: jnp.concatenate([jnp.broadcast_to(ref[...], (128, 512)).T] * 4, 1)
        allowed = (column(kseg_ref) == qseg_ref[...]) & (column(kpos_ref) <= qpos_ref[...])
        mask_ref[...] = jnp.where(allowed, 0.0, MASKED)


def attend_kernel(last, slot_ref, q_ref, kv_ref, qpos_ref, qseg_ref, kpos_ref, kseg_ref, *refs):
    mask_ref = refs[-1]
    set_mask(mask_ref, qpos_ref, qseg_ref, kpos_ref, kseg_ref)
    before, stats_before, out_ref, stats_ref = refs[:4] if last else (None, None, *refs[:2])
    turned = kv_ref[...].T
    outs = []
    for h in range(2):
        q = q_ref[:, h * 64 : h * 64 + 64] * jnp.asarray(0.125, bf16)
        s = dot_nt(kv_ref[:, :64], q) + mask_ref[...]
        top = jnp.max(s, 0, keepdims=True)
        p = jnp.exp(s - top)
        total = jnp.sum(p, 0, keepdims=True)
        out = dot(turned[64:], p.astype(bf16))
        if last:
            top_1, total_1 = stats_before[0, h : h + 1], stats_before[0, 2 + h : 3 + h]
            peak = jnp.maximum(top, top_1)
            scale_1, scale = jnp.exp(top_1 - peak), jnp.exp(top - peak)
            total = scale_1 * total_1 + scale * total
            out = (scale_1 * before[h * 64 : h * 64 + 64] + scale * out) / total
            stats_ref[0, h : h + 1] = peak + jnp.log(total)
        else:
            stats_ref[0, h : h + 1] = top
            stats_ref[0, 2 + h : 3 + h] = total
        outs.append(out)
    out = jnp.concatenate(outs, 0)
    out_ref[...] = out.T.astype(bf16) if last else out


LANES = pl.BlockSpec((512, 128), lambda i, _: (0, i))
GROUP = pl.BlockSpec((512, 128), lambda i, _: (0, i // 2))
TURNED = pl.BlockSpec((128, 512), lambda i, _: (i, 0))
STATS = pl.BlockSpec((1, 8, 512), lambda i, _: (i, 0, 0))


def attend(slots, q, kv, places, before=()):
    last = len(before) > 0
    return pl.pallas_call(
        lambda *refs: attend_kernel(last, *refs),
        out_shape=[
            jax.ShapeDtypeStruct((512, 512), bf16 if last else f32),
            jax.ShapeDtypeStruct((4, 8, 512), f32),
        ],
        name="attend",
        **with_slots(
            4,
            [LANES, GROUP] + [whole(1, 512)] * 4 + [TURNED, STATS] * last,
            [LANES if last else TURNED, STATS],
            [pltpu.VMEM((512, 512), f32)],
        ),
    )(slots, q, kv, *places, *before)


def o_part_kernel(slot_ref, att_ref, wa_ref, wb_ref, *parts):
    for z in range(4):
        lanes = slice(z * 512, (z + 1) * 512)
        o_a = in_order(wa_ref, slot_ref, z, slice(None))
        o_b = in_order(wb_ref, slot_ref, z, slice(None))
        total = dot_nt(att_ref[:, :256], o_a) + dot_nt(att_ref[:, 256:], o_b)
        for ref, start, rows in zip(parts, STARTS, ROWS):
            ref[:, lanes] = total[start : start + rows].astype(bf16)


def o_part_of(slots, attended, w, w2):
    return pl.pallas_call(
        o_part_kernel,
        out_shape=PIECE_SHAPES,
        name="o_part_of",
        **with_slots(1, [whole(512, 512), O_LANES, O_LANES], PIECES),
    )(slots, attended, w, w2)


def d_att_kernel(slot_ref, *refs):
    pieces, (wa_ref, wb_ref, da_ref, d_att_ref) = refs[:5], refs[5:]
    for ref, start, rows in zip(pieces, STARTS, ROWS):
        da_ref[start : start + rows] = ref[...]
    d_att_ref[:, :256] = dot(da_ref[...], weight_of(wa_ref, slot_ref)).astype(bf16)
    d_att_ref[:, 256:] = dot(da_ref[...], weight_of(wb_ref, slot_ref)).astype(bf16)


def d_att_of(slots, pieces, w, w2):
    return pl.pallas_call(
        d_att_kernel,
        out_shape=[jax.ShapeDtypeStruct((512, 2048), bf16), jax.ShapeDtypeStruct((512, 512), bf16)],
        name="d_att_of",
        **with_slots(1, PIECES + [O_LANES, O_LANES], [whole(512, 2048), whole(512, 512)], mib=56),
    )(slots, *pieces, w, w2)


def attend_back_kernel(last, slot_ref, q_ref, kv_ref, qpos_ref, qseg_ref, kpos_ref, kseg_ref, *refs):
    g_ref, att_ref, stats_ref, *refs = refs
    before, cos_ref, sin_ref, dq_ref, dkv_ref = refs[:5] if last else (None, None, None, *refs[:2])
    mask_ref, sum_ref = refs[-2:]
    set_mask(mask_ref, qpos_ref, qseg_ref, kpos_ref, kseg_ref)
    turned = kv_ref[...].T
    inner = (g_ref[...].astype(f32) * att_ref[...].astype(f32)).T
    dqs = []
    dk = jnp.zeros((512, 64), f32)
    dv = jnp.zeros((512, 64), f32)
    for h in range(2):
        lanes = slice(h * 64, h * 64 + 64)
        q = q_ref[:, lanes] * jnp.asarray(0.125, bf16)
        g = g_ref[:, lanes]
        p = jnp.exp(dot_nt(kv_ref[:, :64], q) + mask_ref[...] - stats_ref[0, h : h + 1])
        dp = dot_nt(kv_ref[:, 64:], g)
        ds = (p * (dp - jnp.sum(inner[lanes], 0, keepdims=True))).astype(bf16)
        dk += dot(ds, q)
        dv += dot(p.astype(bf16), g)
        dqs.append(dot(turned[:64], ds))
    new = jnp.concatenate([dk, dv], 1)

    @pl.when(pl.program_id(0) % 2 == 0)
    def _():
        sum_ref[...] = new

    @pl.when(pl.program_id(0) % 2 == 1)
    def _():
        sum_ref[...] += new

    dkv_ref[...] = sum_ref[...].astype(dkv_ref.dtype)
    dq = jnp.concatenate(dqs, 0)
    if last:
        dq = ((dq + before[...]) * 0.125).T
        dq_ref[...] = rotate_back(dq, cos_ref[...], sin_ref[...]).astype(bf16)
    else:
        dq_ref[...] = dq


def attend_back(slots, q, kv, places, g, attended, stats, before=(), tables=()):
    last = len(tables) > 0
    return pl.pallas_call(
        lambda *refs: attend_back_kernel(last, *refs),
        out_shape=[
            jax.ShapeDtypeStruct((512, 512), bf16 if last else f32),
            jax.ShapeDtypeStruct((512, 256), f32 if last else bf16),
        ],
        name="attend_back",
        **with_slots(
            4,
            [LANES, GROUP]
            + [whole(1, 512)] * 4
            + [LANES, LANES, STATS]
            + [TURNED, whole(512, 128), whole(512, 128)] * last,
            [LANES if last else TURNED, GROUP],
            [pltpu.VMEM((512, 512), f32), pltpu.VMEM((512, 128), f32)],
        ),
    )(slots, q, kv, *places, g, attended, stats, *before, *tables)


def d_h1_kernel(slot_ref, dq_ref, dkv_ref, dkv2_ref, cos_ref, sin_ref, qa_ref, qb_ref, kva_ref, kvb_ref, *refs):
    (da_ref, db_ref), parts = refs[:2], refs[2:]
    d_kv = dkv_ref[...] + dkv2_ref[...].astype(f32)
    dk = rotate_back(jnp.concatenate([d_kv[:, :64], d_kv[:, 128:192]], 1), cos_ref[...], sin_ref[...])
    da_ref[...] = jnp.concatenate([dk[:, :64], d_kv[:, 64:128]], 1).astype(bf16)
    db_ref[...] = jnp.concatenate([dk[:, 64:], d_kv[:, 192:]], 1).astype(bf16)
    for z in range(4):
        lanes = slice(z * 512, (z + 1) * 512)
        total = (
            dot_nt(dq_ref[:, :256], in_order(qa_ref, slot_ref, z, slice(None)))
            + dot_nt(dq_ref[:, 256:], in_order(qb_ref, slot_ref, z, slice(None)))
            + dot_nt(da_ref[...], in_order(kva_ref, slot_ref, z, slice(None)))
            + dot_nt(db_ref[...], in_order(kvb_ref, slot_ref, z, slice(None)))
        )
        for part, start, rows in zip(parts, STARTS, ROWS):
            part[:, lanes] = total[start : start + rows].astype(bf16)


def d_h1_of(slots, dq, d_kv, d_kv2, cos, sin, w, w2):
    return pl.pallas_call(
        d_h1_kernel,
        out_shape=[
            jax.ShapeDtypeStruct((512, 128), bf16),
            jax.ShapeDtypeStruct((512, 128), bf16),
        ]
        + PIECE_SHAPES,
        name="d_h1_of",
        **with_slots(
            1,
            [whole(512, 512), whole(512, 256), whole(512, 256), whole(512, 128), whole(512, 128)]
            + [Q_LANES, Q_LANES, KV_LANES, KV_LANES],
            [whole(512, 128), whole(512, 128)] + PIECES,
            mib=28,
        ),
    )(slots, dq, d_kv, d_kv2, cos, sin, w, w2, w, w2)


def inverse_rms(v):
    return lax.rsqrt(jnp.mean(v * v, -1, keepdims=True) + NORM_EPS)


def norm_back(grad_normed, inputs, inv_rms, gain):
    scaled = grad_normed * gain
    return inv_rms * scaled - inputs * inv_rms**3 * jnp.mean(scaled * inputs, -1, keepdims=True)


UNITS = 768
PARTS = 3 * UNITS


def hidden_kernel(first, slot_ref, *refs):
    if first:
        pieces, refs = refs[:5], refs[5:]
        h2_ref = refs[-1]

        @pl.when(pl.program_id(0) == 0)
        def _():
            for ref, start, rows in zip(pieces, STARTS, ROWS):
                h2_ref[start : start + rows] = ref[...]

    else:
        h2_ref, refs = refs[0], refs[1:]
    ct_ref, gate_ref, up_ref, down_ref, hid_ref, dg_ref, du_ref = refs[:7]
    gate = dot(h2_ref[...], weight_of(gate_ref, slot_ref))
    up = dot(h2_ref[...], weight_of(up_ref, slot_ref))
    d_hidden = dot(ct_ref[...], weight_of(down_ref, slot_ref))
    sig = jax.nn.sigmoid(gate)
    act = gate * sig
    hid_ref[...] = (act * up).astype(bf16)
    dg_ref[...] = (d_hidden * up * sig * (1.0 + gate * (1.0 - sig))).astype(bf16)
    du_ref[...] = (d_hidden * act).astype(bf16)


def hidden_of(slots, h2, ct, rows):
    first = isinstance(h2, tuple)
    part = lambda p: pl.BlockSpec((4, 2, 2, 4, 32, 256), lambda i, _: (0, 0, 0, 0, 0, p * 3 + i))
    out = pl.BlockSpec((512, 256), lambda i, _: (0, i))
    view = rows.reshape(4, 2, 2, 4, 32, PARTS)
    return pl.pallas_call(
        lambda *refs: hidden_kernel(first, *refs),
        out_shape=[jax.ShapeDtypeStruct((512, UNITS), bf16)] * 3
        + [jax.ShapeDtypeStruct((512, 2048), bf16)] * first,
        name="hidden_of",
        **with_slots(
            3,
            (PIECES if first else [whole(512, 2048)]) + [whole(512, 2048)] + [part(p) for p in range(3)],
            [out] * 3 + [whole(512, 2048)] * first,
            mib=56,
        ),
    )(slots, *(h2 if first else (h2,)), ct, view, view, view)


def back_kernel(count, slot_ref, *refs):
    acts, weights, outs = refs[: 2 * count], refs[2 * count : 2 * count + 2], refs[2 * count + 2 :]
    total = None
    for s in range(2):
        for k in range(count):
            lanes = slice(k * UNITS, (k + 1) * UNITS)
            term = dot_nt(acts[s * count + k][...], in_order(weights[s], slot_ref, 0, lanes))
            total = term if total is None else total + term
    for ref, start, rows in zip(outs, STARTS, ROWS):
        ref[...] = total[start : start + rows].astype(bf16)


def back_through(slots, acts, rows, rows2, first):
    count = len(acts) // 2
    acts_spec = pl.BlockSpec((512, UNITS), lambda z, _: (0, 0))
    weight = pl.BlockSpec((1, 2, 2, 4, 32, count * UNITS), lambda z, _: (z, 0, 0, 0, 0, first // count))
    view = lambda r: r.reshape(4, 2, 2, 4, 32, PARTS)
    return pl.pallas_call(
        lambda *refs: back_kernel(count, *refs),
        grid_spec=pltpu.PrefetchScalarGridSpec(
            num_scalar_prefetch=1,
            grid=(4,),
            in_specs=[acts_spec] * (2 * count) + [weight] * 2,
            out_specs=[pl.BlockSpec((r, 512), lambda z, _: (0, z)) for r in ROWS],
        ),
        out_shape=[jax.ShapeDtypeStruct((r, 2048), bf16) for r in ROWS],
        compiler_params=pltpu.CompilerParams(vmem_limit_bytes=(56 if count > 1 else 22) << 20),
        cost_estimate=LIGHT,
        name="back_through",
    )(slots, *acts, view(rows), view(rows2))


def grad_kernel(lefts, widths, with_other, slot_ref, *refs):
    out_ref = refs[-1]
    left_refs, rights = refs[: max(lefts) + 1], refs[max(lefts) + 1 :]
    other_ref = rights[len(lefts)] if with_other else None
    turned = [ref[...].T for ref in left_refs]
    start = 0
    for k, width in enumerate(widths):
        lanes = slice(start, start + width)
        grad = dot(turned[lefts[k]], rights[k][...])
        at = 0
        for xl in range(2):
            for y in range(4):
                for xh in range(2):
                    rows = grad[at : at + 32]
                    if other_ref is not None:
                        rows = rows + other_ref[0, xh, xl, slot_ref[y], :, lanes].astype(f32)
                    out_ref[0, xh, xl, slot_ref[y], :, lanes] = rows.astype(bf16)
                    at += 32
        start += width


def weight_grads(slots, left, rights, other=None):
    widths = [width for _, _, _, width in rights]
    total = sum(widths)
    features = pl.BlockSpec((512, 512), lambda z, _: (0, z))
    block = pl.BlockSpec((1, 2, 2, 4, 32, total), lambda z, _: (z, 0, 0, 0, 0, 0))
    lane_block = lambda at, width: pl.BlockSpec((512, width), lambda z, _: (0, at // width))
    specs = [features] * len(left) + [lane_block(at, width) for _, _, at, width in rights]
    args = list(left) + [a for _, a, _, _ in rights]
    if other is not None:
        specs.append(block)
        args.append(other)
    lefts = [k for k, _, _, _ in rights]
    return pl.pallas_call(
        lambda *refs: grad_kernel(lefts, widths, other is not None, *refs),
        out_shape=jax.ShapeDtypeStruct((4, 2, 2, 4, 32, total), bf16),
        name="weight_grads",
        **with_slots(4, specs, block, mib=56 if total == PARTS else 28),
    )(slots, *args)


def layer(
    tokens,
    segment_ids,
    cotangent,
    norm1_gain,
    q_weight,
    k_weight,
    v_weight,
    o_weight,
    norm2_gain,
    gate_weight,
    up_weight,
    down_weight,
):
    y = lax.axis_index("y")
    xh = lax.axis_index("xh")
    core = lax.axis_index("c")
    own = lambda a: lax.dynamic_index_in_dim(a, core, 0, False)
    x_own = own(tokens)
    ct_own = own(cotangent)
    qpos = positions_of(y, xh)
    cos, sin = rope_tables(qpos)
    qpos = qpos.astype(f32)[None]
    far_pos = positions_of(y, 1 - xh).astype(f32)[None]
    x_near = gather_near(x_own, "y")

    split = lambda a: a.reshape(32, 4, -1)
    padded = lambda a: jnp.pad(split(a), ((0, 0), (0, 0), (0, UNITS - 704)))
    twice = lambda a: jnp.repeat(a.reshape(32, 2, 64), 2, axis=1)
    notes = jnp.concatenate([norm1_gain, norm2_gain, jnp.zeros((64,), bf16)])
    notes = jnp.stack([notes, own(segment_ids).astype(bf16)], 0)
    notes = jnp.broadcast_to(jnp.pad(notes, ((0, 30), (0, 0)))[:, None], (32, 4, 128))
    attn = jnp.concatenate(
        [split(q_weight), split(o_weight), twice(k_weight), twice(v_weight), notes], -1
    ).transpose(1, 0, 2)
    mlp = jnp.concatenate([padded(gate_weight), padded(up_weight), padded(down_weight)], -1).transpose(1, 0, 2)

    def by_slot(block):
        pick = lambda d: lax.dynamic_index_in_dim(block, (y + d) % 4, 0, False)
        return jnp.stack([pick(0)] + [shift(pick(-off), "y", -off) for off in OFFSETS[1:]], 0)

    slots = jnp.array((0, 2, 3, 1), jnp.int32)[(jnp.arange(4, dtype=jnp.int32) - y) % 4]
    slots = jnp.concatenate([slots, jnp.stack([lax.axis_index("z"), lax.axis_index("xl"), xh])])
    to_torus = lambda a: lax.all_to_all(a, TORUS, 0, 0, tiled=True)
    six = lambda a: a.reshape(4, 2, 2, 4, 32, -1)
    attn = by_slot(attn).reshape(1, 128, 768)
    attn, mlp, cos, sin, slots, qpos, far_pos = together(attn, mlp, cos, sin, slots, qpos, far_pos)
    mlp = by_slot(mlp)
    w_attn = to_torus(jnp.broadcast_to(attn, (16, 128, 768)))
    x_far = gather_far(x_near, "y")
    ct_near = gather_near(ct_own, "y")
    x_far, ct_near = together(x_far, ct_near)
    w_attn, mlp, x_far, ct_near = together(w_attn, mlp, x_far, ct_near)
    mlp_rows = gather_torus(mlp)
    w_attn2 = six(shift(w_attn, "c", 1))
    w_attn = six(w_attn)

    x_pieces = (x_own, *x_near, *x_far)
    h1, inv_one, kv, gains, ids = project_kv(slots, x_pieces, w_attn, w_attn2, cos, sin)
    h1, kv = together(h1, kv)
    kv2 = shift(kv, "xh", 1)
    queries = project_q(slots, h1, w_attn, w_attn2, cos, sin)
    own_places = (qpos, ids[:1], qpos, ids[:1])
    far_places = (qpos, ids[:1], far_pos, ids[1:])
    first = attend(slots, queries, kv, own_places)
    first, kv2 = together(first, kv2)
    attended, stats = attend(slots, queries, kv2, far_places, first)
    o_part = o_part_of(slots, attended, w_attn, w_attn2)
    o_far = sum_far(o_part, "y")
    o_pass = sum_pass(o_part, o_far)
    o_near = sum_near(o_pass, "y")
    o_pass, ct_near = together(o_pass, ct_near)
    ct_far = gather_far(ct_near, "y")
    ct_all = gathered(ct_own, ct_near, ct_far)
    o_near, ct_all = together(o_near, ct_all)
    middle = x_own.astype(f32) + sum_of(o_part, o_near)

    inv_two = inverse_rms(middle)
    h2_own = (middle * inv_two * gains[1]).astype(bf16)
    h2_near = gather_near(h2_own, "y")
    mlp_rows, h2_near = together(mlp_rows, h2_near)
    mlp_rows2 = shift(mlp_rows, "c", 1)
    h2_pieces = (h2_own, *h2_near, *gather_far(h2_near, "y"))
    hid_a, dg_a, du_a, h2 = hidden_of(slots, h2_pieces, ct_all, mlp_rows)
    hid_b, dg_b, du_b = hidden_of(slots, h2, ct_all, mlp_rows2)

    def mlp_grads(h2, hid, dg, du, other=None):
        rights = [(0, dg, 0, UNITS), (0, du, 0, UNITS), (1, hid, 0, UNITS)]
        return weight_grads(slots, (h2, ct_all), rights, other)

    grads_b = mlp_grads(h2, hid_b, dg_b, du_b)
    grads_b, dg_a, du_a = together(grads_b, dg_a, du_a)
    grads_b2 = shift(grads_b, "c", 1)
    d_h2_part = back_through(slots, (dg_a, du_a, dg_b, du_b), mlp_rows, mlp_rows2, 0)
    d_h2_far = sum_far(d_h2_part, "y")
    d_h2_pass = sum_pass(d_h2_part, d_h2_far)
    d_h2_pass, h2 = together(d_h2_pass, h2)
    d_h2_near = sum_near(d_h2_pass, "y")
    mlp_grad = mlp_grads(h2, hid_a, dg_a, du_a, grads_b2)
    d_h2_near, mlp_grad = together(d_h2_near, mlp_grad)
    d_h2 = sum_of(d_h2_part, d_h2_near)
    d_middle = ct_own.astype(f32) + norm_back(d_h2, middle, inv_two, gains[1])
    da_own = d_middle.astype(bf16)
    da_near = gather_near(da_own, "y")
    out_part = back_through(slots, (hid_a, hid_b), mlp_rows, mlp_rows2, 2)
    da_near, out_part = together(da_near, out_part)
    da_far = gather_far(da_near, "y")
    da_pieces = (da_own, *da_near, *da_far)

    da, d_att = d_att_of(slots, da_pieces, w_attn, w_attn2)
    dq_far, d_kv2 = attend_back(slots, queries, kv2, far_places, d_att, attended, stats)
    d_kv2 = shift(d_kv2, "xh", 1)
    dq, d_kv = attend_back(
        slots, queries, kv, own_places, d_att, attended, stats, (dq_far,), (cos, sin)
    )
    dq, d_kv, d_kv2 = together(dq, d_kv, d_kv2)
    dkv_a, dkv_b, *d_h1_part = d_h1_of(slots, dq, d_kv, d_kv2, cos, sin, w_attn, w_attn2)
    d_h1_part, h1 = together(d_h1_part, h1)
    d_h1_far = sum_far(d_h1_part, "y")
    def attn_grads(h1, at, dkv, other=None):
        rights = [(0, dq, at, 256), (1, attended, at, 256), (0, dkv, 0, 128)]
        return weight_grads(slots, (h1, da), rights, other)

    grads_2 = attn_grads(h1, 256, dkv_b)
    d_h1_far, grads_2 = together(d_h1_far, grads_2)
    grads_2 = shift(grads_2, "c", 1)
    d_h1_near = sum_near(sum_pass(d_h1_part, d_h1_far), "y")
    grads_1 = attn_grads(h1, 0, dkv_a, grads_2)
    mlp_own = lax.psum_scatter(mlp_grad.reshape(2048, PARTS), TORUS, scatter_dimension=0, tiled=True)
    grads_1, d_h1_near, mlp_own = together(grads_1, d_h1_near, mlp_own)
    got = to_torus(grads_1.reshape(16, 128, 640))
    def to_y(grads):
        ring = [shift(grads[1], "y", -1), shift(grads[3], "y", 2), shift(grads[2], "y", 1), grads[0]]
        ring = jnp.stack(ring + ring[:3], 0)
        return lax.dynamic_slice_in_dim(ring, 3 - y, 4, 0).astype(f32)

    columns = lambda got: got.transpose(1, 0, 2).reshape(32, -1)
    grads = to_y(mlp_own.reshape(4, 32, PARTS))
    own_gate, own_up, own_down = (columns(grads[:, :, p * UNITS : p * UNITS + 704]) for p in range(3))
    d_h1 = sum_of(d_h1_part, d_h1_near)
    dx_own = (d_middle + norm_back(d_h1, x_own.astype(f32), inv_one[:128], gains[0])).astype(bf16)
    mlp_own, out_part = together(mlp_own, out_part)
    out_near = sum_near(sum_pass(out_part, sum_far(out_part, "y")), "y")
    out_own = (middle + sum_of(out_part, out_near)).astype(bf16)

    def both(a):
        other = shift(a, "c", 1)
        return jnp.where(core == 0, jnp.stack([a, other]), jnp.stack([other, a]))

    out, dx = both(out_own), both(dx_own)
    got, own_gate, own_up, own_down, out, dx = together(got, own_gate, own_up, own_down, out, dx)
    grads = to_y(got.astype(f32).sum(0).astype(bf16).reshape(4, 32, 640))
    own_q, own_o, own_kv = grads[:, :, :256], grads[:, :, 256:512], grads[:, :, 512:640]
    pair = lambda a: a.reshape(2, 2, 32, 64).sum(1).transpose(1, 0, 2).reshape(32, 128)
    own_q, own_o = columns(own_q), columns(own_o)
    own_k, own_v = pair(own_kv[:, :, :64]), pair(own_kv[:, :, 64:])

    def gain_grad(gain, *pairs):
        mine = sum(jnp.sum(w.astype(f32) * g, 1) for w, g in pairs)
        return (mine + shift(mine, "c", 1)) / gain.astype(f32)

    gain_two_grad = gain_grad(norm2_gain, (gate_weight, own_gate), (up_weight, own_up))
    gain_one_grad = gain_grad(norm1_gain, (q_weight, own_q), (k_weight, own_k), (v_weight, own_v))

    return (
        out,
        dx,
        gain_one_grad,
        own_q,
        own_k,
        own_v,
        own_o,
        gain_two_grad,
        own_gate,
        own_up,
        own_down,
    )


def solution(mesh):
    fine = Mesh(mesh.devices.reshape(4, 2, 4, 2, 2), ("z", "xl", "y", "xh", "c"))
    fsdp, cp = ("z", "xl"), ("y", "xh")
    acts, gain, weight = P(fsdp, cp, None), P(fsdp + cp), P(fsdp + cp, "c")
    return jax.shard_map(
        layer,
        mesh=fine,
        in_specs=(acts, P(fsdp, cp), acts, gain, weight, weight, weight, weight, gain, weight, weight, weight),
        out_specs=(acts, acts, gain, weight, weight, weight, weight, gain, weight, weight, weight),
        check_vma=False,
    )
```

```python
import jax
import jax.numpy as jnp
from jax import lax
from jax.experimental import pallas as pl
from jax.experimental.pallas import tpu as pltpu
from jax.sharding import Mesh
from jax.sharding import PartitionSpec as P

HEAD_DIM = 64
NORM_EPS = 1e-05
ROPE_BASE = 10000.0
X_RING = ("xl", "xh")
OFFSETS = (0, -1, 1, 2)
LIGHT = pl.CostEstimate(flops=1 << 20, bytes_accessed=1 << 16, transcendentals=0)
bf16 = jnp.bfloat16
f32 = jnp.float32


def x_index(x):
    return (x % 2) * 2 + x // 2


def shift(v, ring, d):
    if ring == X_RING:
        return lax.ppermute(v, X_RING, [(x_index(i), x_index((i + d) % 4)) for i in range(4)])
    n = 2 if ring in ("c", "xh") else 4
    return lax.ppermute(v, ring, [(i, (i + d) % n) for i in range(n)])


def gather_near(v, ring):
    return shift(v, ring, 1), shift(v, ring, -1)


def gather_far(near, ring):
    left, right = near
    half = left.shape[0] // 2
    return shift(left[:half], ring, 1), shift(right[half:], ring, -1)


def gathered(v, near, far):
    return jnp.concatenate([v, *near, *far], 0)


def sum_far(parts, ring):
    return shift(parts[3], ring, 1), shift(parts[4], ring, -1)


def sum_pass(parts, far):
    half = parts[3].shape[0]
    left, right = parts[1], parts[2]
    up = jnp.concatenate([(right[:half].astype(f32) + far[0].astype(f32)).astype(bf16), right[half:]], 0)
    down = jnp.concatenate([left[:half], (left[half:].astype(f32) + far[1].astype(f32)).astype(bf16)], 0)
    return up, down


def sum_near(passed, ring):
    return shift(passed[0], ring, 1), shift(passed[1], ring, -1)


def sum_of(parts, near):
    return parts[0].astype(f32) + near[0].astype(f32) + near[1].astype(f32)


def together(*values):
    return lax.optimization_barrier(values)


TORUS = ("z", "xh", "xl")


def gather_torus(block):
    n = block.shape[-1]
    return lax.all_gather(block.reshape(128, n), TORUS, axis=0, tiled=True)


def positions_of(y, xh):
    rows = []
    o = jnp.arange(64, dtype=jnp.int32)
    for off in OFFSETS:
        i = ((y + off) % 4) * 2 + xh
        rows += [i * 64 + o, (15 - i) * 64 + o]
    return jnp.concatenate(rows)


def rope_tables(positions):
    inverse = ROPE_BASE ** (-jnp.arange(0, HEAD_DIM // 2, dtype=f32) * 2.0 / HEAD_DIM)
    angles = positions.astype(f32)[:, None] * inverse[None, :]
    cos = jnp.cos(angles)
    sin = jnp.sin(angles)
    return jnp.concatenate([cos] * 4, -1), jnp.concatenate([-sin, sin] * 2, -1)


def swap_halves(u):
    lane = lax.broadcasted_iota(jnp.int32, u.shape, 1)
    return jnp.where(lane % HEAD_DIM < HEAD_DIM // 2, pltpu.roll(u, u.shape[1] - 32, 1), pltpu.roll(u, 32, 1))


def wide(table, width):
    return jnp.concatenate([table] * (width // 128), 1)


def rotate(u, cos, sin):
    w = u.shape[1]
    return u * wide(cos, w) + swap_halves(u) * wide(sin, w)


def rotate_back(w, cos, sin):
    n = w.shape[1]
    return w * wide(cos, n) + swap_halves(w * wide(sin, n))


def dot(a, b):
    return jnp.dot(a, b, preferred_element_type=f32)


def dot_nt(a, b):
    return lax.dot_general(a, b, (((1,), (1,)), ((), ())), preferred_element_type=f32)


def dot_tn(a, b):
    return lax.dot_general(a, b, (((0,), (0,)), ((), ())), preferred_element_type=f32)


ROWS = (128, 128, 128, 64, 64)
STARTS = (0, 128, 256, 384, 448)
Q_LANES = pl.BlockSpec((4, 2, 2, 4, 32, 256), lambda *_: (0,) * 6)
O_LANES = pl.BlockSpec((4, 2, 2, 4, 32, 256), lambda *_: (0, 0, 0, 0, 0, 1))
KV_LANES = pl.BlockSpec((4, 2, 2, 4, 32, 128), lambda *_: (0, 0, 0, 0, 0, 4))
NOTE_LANES = pl.BlockSpec((4, 2, 2, 4, 32, 128), lambda *_: (0, 0, 0, 0, 0, 5))
MASKED = -1e30
PIECES = [pl.BlockSpec((r, 2048), lambda *_: (0, 0)) for r in ROWS]
PIECE_SHAPES = [jax.ShapeDtypeStruct((r, 2048), bf16) for r in ROWS]


def whole(*shape):
    return pl.BlockSpec(shape, lambda *_: (0,) * len(shape))


def in_order(ref, slot_ref, z, lanes):
    return jnp.concatenate(
        [ref[z, xh, xl, slot_ref[y], :, lanes] for xl in range(2) for y in range(4) for xh in range(2)], 0
    )


def weight_of(ref, slot_ref):
    return jnp.concatenate([in_order(ref, slot_ref, z, slice(None)) for z in range(4)], 0)


def project_kv_kernel(slot_ref, *refs):
    pieces, refs = refs[:5], refs[5:]
    note_ref, wa_ref, wb_ref, cos_ref, sin_ref, h1_ref, inv_ref, kv_ref, gain_ref, seg_ref = refs
    notes = lambda at: jnp.concatenate(
        [
            note_ref[z, xh, xl, slot_ref[y], 0:1, at : at + 32]
            for z in range(4)
            for xl in range(2)
            for y in range(4)
            for xh in range(2)
        ],
        1,
    ).astype(f32)
    gain_ref[0:1] = notes(0)
    gain_ref[1:2] = notes(32)
    z, xl, xh = slot_ref[4], slot_ref[5], slot_ref[6]
    for k in range(2):
        row = [note_ref[z, (xh + k) % 2, xl, j, 1:2, :] for j in range(4)]
        seg_ref[k : k + 1] = jnp.concatenate(row, 1).astype(f32)
    for ref, start, rows in zip(pieces, STARTS, ROWS):
        x = ref[...].astype(f32)
        inv = lax.rsqrt(jnp.mean(x * x, -1, keepdims=True) + NORM_EPS)
        inv_ref[start : start + rows] = inv
        h1_ref[start : start + rows] = (x * inv * gain_ref[0:1]).astype(bf16)
    a = dot(h1_ref[...], weight_of(wa_ref, slot_ref))
    b = dot(h1_ref[...], weight_of(wb_ref, slot_ref))
    keys = rotate(jnp.concatenate([a[:, :64], b[:, :64]], 1), cos_ref[...], sin_ref[...])
    kv_ref[...] = jnp.concatenate([keys[:, :64], a[:, 64:], keys[:, 64:], b[:, 64:]], 1).astype(bf16)


def with_slots(grid, in_specs, out_specs, scratch=(), mib=16):
    return dict(
        grid_spec=pltpu.PrefetchScalarGridSpec(
            num_scalar_prefetch=1, grid=(grid,), in_specs=in_specs, out_specs=out_specs, scratch_shapes=scratch
        ),
        compiler_params=pltpu.CompilerParams(vmem_limit_bytes=mib << 20),
        cost_estimate=LIGHT,
    )


def project_kv(slots, pieces, w, w2, cos, sin):
    return pl.pallas_call(
        project_kv_kernel,
        out_shape=[
            jax.ShapeDtypeStruct((512, 2048), bf16),
            jax.ShapeDtypeStruct((512, 1), f32),
            jax.ShapeDtypeStruct((512, 256), bf16),
            jax.ShapeDtypeStruct((2, 2048), f32),
            jax.ShapeDtypeStruct((2, 512), f32),
        ],
        name="project_kv",
        **with_slots(
            1,
            PIECES + [NOTE_LANES, KV_LANES, KV_LANES, whole(512, 128), whole(512, 128)],
            [whole(512, 2048), whole(512, 1), whole(512, 256), whole(2, 2048), whole(2, 512)],
            mib=56,
        ),
    )(slots, *pieces, w, w, w2, cos, sin)


def project_q_kernel(slot_ref, h1_ref, wa_ref, wb_ref, cos_ref, sin_ref, q_ref):
    for k, w_ref in enumerate((wa_ref, wb_ref)):
        q = rotate(dot(h1_ref[...], weight_of(w_ref, slot_ref)), cos_ref[...], sin_ref[...])
        q_ref[:, k * 256 : (k + 1) * 256] = q.astype(bf16)


def project_q(slots, h1, w, w2, cos, sin):
    rows = lambda n: pl.BlockSpec((256, n), lambda i, _: (i, 0))
    return pl.pallas_call(
        project_q_kernel,
        out_shape=jax.ShapeDtypeStruct((512, 512), bf16),
        name="project_q",
        **with_slots(2, [rows(2048), Q_LANES, Q_LANES, rows(128), rows(128)], rows(512), mib=56),
    )(slots, h1, w, w2, cos, sin)


def set_mask(mask_ref, qpos_ref, qseg_ref, kpos_ref, kseg_ref):
    @pl.when(pl.program_id(0) == 0)
    def _():
        column = lambda ref: jnp.concatenate([jnp.broadcast_to(ref[...], (128, 512)).T] * 4, 1)
        allowed = (column(kseg_ref) == qseg_ref[...]) & (column(kpos_ref) <= qpos_ref[...])
        mask_ref[...] = jnp.where(allowed, 0.0, MASKED)


def attend_kernel(last, slot_ref, q_ref, kv_ref, qpos_ref, qseg_ref, kpos_ref, kseg_ref, *refs):
    mask_ref = refs[-1]
    set_mask(mask_ref, qpos_ref, qseg_ref, kpos_ref, kseg_ref)
    before, stats_before, out_ref, stats_ref = refs[:4] if last else (None, None, *refs[:2])
    turned = kv_ref[...].T
    outs = []
    for h in range(2):
        q = q_ref[:, h * 64 : h * 64 + 64] * jnp.asarray(0.125, bf16)
        s = dot_nt(kv_ref[:, :64], q) + mask_ref[...]
        top = jnp.max(s, 0, keepdims=True)
        p = jnp.exp(s - top)
        total = jnp.sum(p, 0, keepdims=True)
        out = dot(turned[64:], p.astype(bf16))
        if last:
            top_1, total_1 = stats_before[0, h : h + 1], stats_before[0, 2 + h : 3 + h]
            peak = jnp.maximum(top, top_1)
            scale_1, scale = jnp.exp(top_1 - peak), jnp.exp(top - peak)
            total = scale_1 * total_1 + scale * total
            out = (scale_1 * before[h * 64 : h * 64 + 64] + scale * out) / total
            stats_ref[0, h : h + 1] = peak + jnp.log(total)
        else:
            stats_ref[0, h : h + 1] = top
            stats_ref[0, 2 + h : 3 + h] = total
        outs.append(out)
    out = jnp.concatenate(outs, 0)
    out_ref[...] = out.T.astype(bf16) if last else out


LANES = pl.BlockSpec((512, 128), lambda i, _: (0, i))
GROUP = pl.BlockSpec((512, 128), lambda i, _: (0, i // 2))
TURNED = pl.BlockSpec((128, 512), lambda i, _: (i, 0))
STATS = pl.BlockSpec((1, 8, 512), lambda i, _: (i, 0, 0))


def attend(slots, q, kv, places, before=()):
    last = len(before) > 0
    return pl.pallas_call(
        lambda *refs: attend_kernel(last, *refs),
        out_shape=[
            jax.ShapeDtypeStruct((512, 512), bf16 if last else f32),
            jax.ShapeDtypeStruct((4, 8, 512), f32),
        ],
        name="attend",
        **with_slots(
            4,
            [LANES, GROUP] + [whole(1, 512)] * 4 + [TURNED, STATS] * last,
            [LANES if last else TURNED, STATS],
            [pltpu.VMEM((512, 512), f32)],
        ),
    )(slots, q, kv, *places, *before)


def o_part_kernel(slot_ref, att_ref, wa_ref, wb_ref, *parts):
    for z in range(4):
        lanes = slice(z * 512, (z + 1) * 512)
        o_a = in_order(wa_ref, slot_ref, z, slice(None))
        o_b = in_order(wb_ref, slot_ref, z, slice(None))
        total = dot_nt(att_ref[:, :256], o_a) + dot_nt(att_ref[:, 256:], o_b)
        for ref, start, rows in zip(parts, STARTS, ROWS):
            ref[:, lanes] = total[start : start + rows].astype(bf16)


def o_part_of(slots, attended, w, w2):
    return pl.pallas_call(
        o_part_kernel,
        out_shape=PIECE_SHAPES,
        name="o_part_of",
        **with_slots(1, [whole(512, 512), O_LANES, O_LANES], PIECES),
    )(slots, attended, w, w2)


def d_att_kernel(slot_ref, *refs):
    pieces, (wa_ref, wb_ref, da_ref, d_att_ref) = refs[:5], refs[5:]
    for ref, start, rows in zip(pieces, STARTS, ROWS):
        da_ref[start : start + rows] = ref[...]
    d_att_ref[:, :256] = dot(da_ref[...], weight_of(wa_ref, slot_ref)).astype(bf16)
    d_att_ref[:, 256:] = dot(da_ref[...], weight_of(wb_ref, slot_ref)).astype(bf16)


def d_att_of(slots, pieces, w, w2):
    return pl.pallas_call(
        d_att_kernel,
        out_shape=[jax.ShapeDtypeStruct((512, 2048), bf16), jax.ShapeDtypeStruct((512, 512), bf16)],
        name="d_att_of",
        **with_slots(1, PIECES + [O_LANES, O_LANES], [whole(512, 2048), whole(512, 512)], mib=56),
    )(slots, *pieces, w, w2)


def attend_back_kernel(last, slot_ref, q_ref, kv_ref, qpos_ref, qseg_ref, kpos_ref, kseg_ref, *refs):
    g_ref, att_ref, stats_ref, *refs = refs
    before, cos_ref, sin_ref, dq_ref, dkv_ref = refs[:5] if last else (None, None, None, *refs[:2])
    mask_ref, sum_ref = refs[-2:]
    set_mask(mask_ref, qpos_ref, qseg_ref, kpos_ref, kseg_ref)
    turned = kv_ref[...].T
    inner = (g_ref[...].astype(f32) * att_ref[...].astype(f32)).T
    dqs = []
    dk = jnp.zeros((512, 64), f32)
    dv = jnp.zeros((512, 64), f32)
    for h in range(2):
        lanes = slice(h * 64, h * 64 + 64)
        q = q_ref[:, lanes] * jnp.asarray(0.125, bf16)
        g = g_ref[:, lanes]
        p = jnp.exp(dot_nt(kv_ref[:, :64], q) + mask_ref[...] - stats_ref[0, h : h + 1])
        dp = dot_nt(kv_ref[:, 64:], g)
        ds = (p * (dp - jnp.sum(inner[lanes], 0, keepdims=True))).astype(bf16)
        dk += dot(ds, q)
        dv += dot(p.astype(bf16), g)
        dqs.append(dot(turned[:64], ds))
    new = jnp.concatenate([dk, dv], 1)

    @pl.when(pl.program_id(0) % 2 == 0)
    def _():
        sum_ref[...] = new

    @pl.when(pl.program_id(0) % 2 == 1)
    def _():
        sum_ref[...] += new

    dkv_ref[...] = sum_ref[...].astype(dkv_ref.dtype)
    dq = jnp.concatenate(dqs, 0)
    if last:
        dq = ((dq + before[...]) * 0.125).T
        dq_ref[...] = rotate_back(dq, cos_ref[...], sin_ref[...]).astype(bf16)
    else:
        dq_ref[...] = dq


def attend_back(slots, q, kv, places, g, attended, stats, before=(), tables=()):
    last = len(tables) > 0
    return pl.pallas_call(
        lambda *refs: attend_back_kernel(last, *refs),
        out_shape=[
            jax.ShapeDtypeStruct((512, 512), bf16 if last else f32),
            jax.ShapeDtypeStruct((512, 256), f32 if last else bf16),
        ],
        name="attend_back",
        **with_slots(
            4,
            [LANES, GROUP]
            + [whole(1, 512)] * 4
            + [LANES, LANES, STATS]
            + [TURNED, whole(512, 128), whole(512, 128)] * last,
            [LANES if last else TURNED, GROUP],
            [pltpu.VMEM((512, 512), f32), pltpu.VMEM((512, 128), f32)],
        ),
    )(slots, q, kv, *places, g, attended, stats, *before, *tables)


def d_h1_kernel(slot_ref, dq_ref, dkv_ref, dkv2_ref, cos_ref, sin_ref, qa_ref, qb_ref, kva_ref, kvb_ref, *refs):
    (da_ref, db_ref), parts = refs[:2], refs[2:]
    d_kv = dkv_ref[...] + dkv2_ref[...].astype(f32)
    dk = rotate_back(jnp.concatenate([d_kv[:, :64], d_kv[:, 128:192]], 1), cos_ref[...], sin_ref[...])
    da_ref[...] = jnp.concatenate([dk[:, :64], d_kv[:, 64:128]], 1).astype(bf16)
    db_ref[...] = jnp.concatenate([dk[:, 64:], d_kv[:, 192:]], 1).astype(bf16)
    for z in range(4):
        lanes = slice(z * 512, (z + 1) * 512)
        total = (
            dot_nt(dq_ref[:, :256], in_order(qa_ref, slot_ref, z, slice(None)))
            + dot_nt(dq_ref[:, 256:], in_order(qb_ref, slot_ref, z, slice(None)))
            + dot_nt(da_ref[...], in_order(kva_ref, slot_ref, z, slice(None)))
            + dot_nt(db_ref[...], in_order(kvb_ref, slot_ref, z, slice(None)))
        )
        for part, start, rows in zip(parts, STARTS, ROWS):
            part[:, lanes] = total[start : start + rows].astype(bf16)


def d_h1_of(slots, dq, d_kv, d_kv2, cos, sin, w, w2):
    return pl.pallas_call(
        d_h1_kernel,
        out_shape=[
            jax.ShapeDtypeStruct((512, 128), bf16),
            jax.ShapeDtypeStruct((512, 128), bf16),
        ]
        + PIECE_SHAPES,
        name="d_h1_of",
        **with_slots(
            1,
            [whole(512, 512), whole(512, 256), whole(512, 256), whole(512, 128), whole(512, 128)]
            + [Q_LANES, Q_LANES, KV_LANES, KV_LANES],
            [whole(512, 128), whole(512, 128)] + PIECES,
            mib=28,
        ),
    )(slots, dq, d_kv, d_kv2, cos, sin, w, w2, w, w2)


def inverse_rms(v):
    return lax.rsqrt(jnp.mean(v * v, -1, keepdims=True) + NORM_EPS)


def norm_back(grad_normed, inputs, inv_rms, gain):
    scaled = grad_normed * gain
    return inv_rms * scaled - inputs * inv_rms**3 * jnp.mean(scaled * inputs, -1, keepdims=True)


UNITS = 768
PARTS = 3 * UNITS


def hidden_kernel(first, slot_ref, *refs):
    if first:
        pieces, refs = refs[:5], refs[5:]
        h2_ref = refs[-1]

        @pl.when(pl.program_id(0) == 0)
        def _():
            for ref, start, rows in zip(pieces, STARTS, ROWS):
                h2_ref[start : start + rows] = ref[...]

    else:
        h2_ref, refs = refs[0], refs[1:]
    ct_ref, gate_ref, up_ref, down_ref, hid_ref, dg_ref, du_ref = refs[:7]
    gate = dot(h2_ref[...], weight_of(gate_ref, slot_ref))
    up = dot(h2_ref[...], weight_of(up_ref, slot_ref))
    d_hidden = dot(ct_ref[...], weight_of(down_ref, slot_ref))
    sig = jax.nn.sigmoid(gate)
    act = gate * sig
    hid_ref[...] = (act * up).astype(bf16)
    dg_ref[...] = (d_hidden * up * sig * (1.0 + gate * (1.0 - sig))).astype(bf16)
    du_ref[...] = (d_hidden * act).astype(bf16)


def hidden_of(slots, h2, ct, rows):
    first = isinstance(h2, tuple)
    part = lambda p: pl.BlockSpec((4, 2, 2, 4, 32, 256), lambda i, _: (0, 0, 0, 0, 0, p * 3 + i))
    out = pl.BlockSpec((512, 256), lambda i, _: (0, i))
    view = rows.reshape(4, 2, 2, 4, 32, PARTS)
    return pl.pallas_call(
        lambda *refs: hidden_kernel(first, *refs),
        out_shape=[jax.ShapeDtypeStruct((512, UNITS), bf16)] * 3
        + [jax.ShapeDtypeStruct((512, 2048), bf16)] * first,
        name="hidden_of",
        **with_slots(
            3,
            (PIECES if first else [whole(512, 2048)]) + [whole(512, 2048)] + [part(p) for p in range(3)],
            [out] * 3 + [whole(512, 2048)] * first,
            mib=56,
        ),
    )(slots, *(h2 if first else (h2,)), ct, view, view, view)


def back_kernel(count, slot_ref, *refs):
    acts, weights, outs = refs[: 2 * count], refs[2 * count : 2 * count + 2], refs[2 * count + 2 :]
    total = None
    for s in range(2):
        for k in range(count):
            lanes = slice(k * UNITS, (k + 1) * UNITS)
            term = dot_nt(acts[s * count + k][...], in_order(weights[s], slot_ref, 0, lanes))
            total = term if total is None else total + term
    for ref, start, rows in zip(outs, STARTS, ROWS):
        ref[...] = total[start : start + rows].astype(bf16)


def back_through(slots, acts, rows, rows2, first):
    count = len(acts) // 2
    acts_spec = pl.BlockSpec((512, UNITS), lambda z, _: (0, 0))
    weight = pl.BlockSpec((1, 2, 2, 4, 32, count * UNITS), lambda z, _: (z, 0, 0, 0, 0, first // count))
    view = lambda r: r.reshape(4, 2, 2, 4, 32, PARTS)
    return pl.pallas_call(
        lambda *refs: back_kernel(count, *refs),
        grid_spec=pltpu.PrefetchScalarGridSpec(
            num_scalar_prefetch=1,
            grid=(4,),
            in_specs=[acts_spec] * (2 * count) + [weight] * 2,
            out_specs=[pl.BlockSpec((r, 512), lambda z, _: (0, z)) for r in ROWS],
        ),
        out_shape=[jax.ShapeDtypeStruct((r, 2048), bf16) for r in ROWS],
        compiler_params=pltpu.CompilerParams(vmem_limit_bytes=(56 if count > 1 else 22) << 20),
        cost_estimate=LIGHT,
        name="back_through",
    )(slots, *acts, view(rows), view(rows2))


def grad_kernel(lefts, widths, with_other, slot_ref, *refs):
    out_ref = refs[-1]
    left_refs, rights = refs[: max(lefts) + 1], refs[max(lefts) + 1 :]
    other_ref = rights[len(lefts)] if with_other else None
    turned = [ref[...].T for ref in left_refs]
    start = 0
    for k, width in enumerate(widths):
        lanes = slice(start, start + width)
        grad = dot(turned[lefts[k]], rights[k][...])
        at = 0
        for xl in range(2):
            for y in range(4):
                for xh in range(2):
                    rows = grad[at : at + 32]
                    if other_ref is not None:
                        rows = rows + other_ref[0, xh, xl, slot_ref[y], :, lanes].astype(f32)
                    out_ref[0, xh, xl, slot_ref[y], :, lanes] = rows.astype(bf16)
                    at += 32
        start += width


def weight_grads(slots, left, rights, other=None):
    widths = [width for _, _, _, width in rights]
    total = sum(widths)
    features = pl.BlockSpec((512, 512), lambda z, _: (0, z))
    block = pl.BlockSpec((1, 2, 2, 4, 32, total), lambda z, _: (z, 0, 0, 0, 0, 0))
    lane_block = lambda at, width: pl.BlockSpec((512, width), lambda z, _: (0, at // width))
    specs = [features] * len(left) + [lane_block(at, width) for _, _, at, width in rights]
    args = list(left) + [a for _, a, _, _ in rights]
    if other is not None:
        specs.append(block)
        args.append(other)
    lefts = [k for k, _, _, _ in rights]
    return pl.pallas_call(
        lambda *refs: grad_kernel(lefts, widths, other is not None, *refs),
        out_shape=jax.ShapeDtypeStruct((4, 2, 2, 4, 32, total), bf16),
        name="weight_grads",
        **with_slots(4, specs, block, mib=56 if total == PARTS else 28),
    )(slots, *args)


def layer(
    tokens,
    segment_ids,
    cotangent,
    norm1_gain,
    q_weight,
    k_weight,
    v_weight,
    o_weight,
    norm2_gain,
    gate_weight,
    up_weight,
    down_weight,
):
    y = lax.axis_index("y")
    xh = lax.axis_index("xh")
    core = lax.axis_index("c")
    own = lambda a: lax.dynamic_index_in_dim(a, core, 0, False)
    x_own = own(tokens)
    ct_own = own(cotangent)
    qpos = positions_of(y, xh)
    cos, sin = rope_tables(qpos)
    qpos = qpos.astype(f32)[None]
    far_pos = positions_of(y, 1 - xh).astype(f32)[None]
    x_near = gather_near(x_own, "y")

    split = lambda a: a.reshape(32, 4, -1)
    padded = lambda a: jnp.pad(split(a), ((0, 0), (0, 0), (0, UNITS - 704)))
    twice = lambda a: jnp.repeat(a.reshape(32, 2, 64), 2, axis=1)
    notes = jnp.concatenate([norm1_gain, norm2_gain, jnp.zeros((64,), bf16)])
    notes = jnp.stack([notes, own(segment_ids).astype(bf16)], 0)
    notes = jnp.broadcast_to(jnp.pad(notes, ((0, 30), (0, 0)))[:, None], (32, 4, 128))
    attn = jnp.concatenate(
        [split(q_weight), split(o_weight), twice(k_weight), twice(v_weight), notes], -1
    ).transpose(1, 0, 2)
    mlp = jnp.concatenate([padded(gate_weight), padded(up_weight), padded(down_weight)], -1).transpose(1, 0, 2)

    def by_slot(block):
        pick = lambda d: lax.dynamic_index_in_dim(block, (y + d) % 4, 0, False)
        return jnp.stack([pick(0)] + [shift(pick(-off), "y", -off) for off in OFFSETS[1:]], 0)

    slots = jnp.array((0, 2, 3, 1), jnp.int32)[(jnp.arange(4, dtype=jnp.int32) - y) % 4]
    slots = jnp.concatenate([slots, jnp.stack([lax.axis_index("z"), lax.axis_index("xl"), xh])])
    to_torus = lambda a: lax.all_to_all(a, TORUS, 0, 0, tiled=True)
    six = lambda a: a.reshape(4, 2, 2, 4, 32, -1)
    attn = by_slot(attn).reshape(1, 128, 768)
    attn, mlp, cos, sin, slots, qpos, far_pos = together(attn, mlp, cos, sin, slots, qpos, far_pos)
    mlp = by_slot(mlp)
    w_attn = to_torus(jnp.broadcast_to(attn, (16, 128, 768)))
    w_attn2 = six(shift(w_attn, "c", 1))
    x_far = gather_far(x_near, "y")
    ct_near = gather_near(ct_own, "y")
    x_far, ct_near = together(x_far, ct_near)
    w_attn, mlp, x_far, ct_near = together(w_attn, mlp, x_far, ct_near)
    mlp_rows = gather_torus(mlp)
    w_attn = six(w_attn)

    x_pieces = (x_own, *x_near, *x_far)
    h1, inv_one, kv, gains, ids = project_kv(slots, x_pieces, w_attn, w_attn2, cos, sin)
    h1, kv = together(h1, kv)
    kv2 = shift(kv, "xh", 1)
    queries = project_q(slots, h1, w_attn, w_attn2, cos, sin)
    own_places = (qpos, ids[:1], qpos, ids[:1])
    far_places = (qpos, ids[:1], far_pos, ids[1:])
    first = attend(slots, queries, kv, own_places)
    first, kv2 = together(first, kv2)
    attended, stats = attend(slots, queries, kv2, far_places, first)
    o_part = o_part_of(slots, attended, w_attn, w_attn2)
    o_far = sum_far(o_part, "y")
    o_pass = sum_pass(o_part, o_far)
    o_near = sum_near(o_pass, "y")
    o_pass, ct_near = together(o_pass, ct_near)
    ct_far = gather_far(ct_near, "y")
    ct_all = gathered(ct_own, ct_near, ct_far)
    o_near, ct_all = together(o_near, ct_all)
    middle = x_own.astype(f32) + sum_of(o_part, o_near)

    inv_two = inverse_rms(middle)
    h2_own = (middle * inv_two * gains[1]).astype(bf16)
    h2_near = gather_near(h2_own, "y")
    mlp_rows, h2_near = together(mlp_rows, h2_near)
    mlp_rows2 = shift(mlp_rows, "c", 1)
    h2_pieces = (h2_own, *h2_near, *gather_far(h2_near, "y"))
    hid_a, dg_a, du_a, h2 = hidden_of(slots, h2_pieces, ct_all, mlp_rows)
    hid_b, dg_b, du_b = hidden_of(slots, h2, ct_all, mlp_rows2)

    def mlp_grads(h2, hid, dg, du, other=None):
        rights = [(0, dg, 0, UNITS), (0, du, 0, UNITS), (1, hid, 0, UNITS)]
        return weight_grads(slots, (h2, ct_all), rights, other)

    grads_b = mlp_grads(h2, hid_b, dg_b, du_b)
    grads_b, dg_a, du_a = together(grads_b, dg_a, du_a)
    grads_b2 = shift(grads_b, "c", 1)
    d_h2_part = back_through(slots, (dg_a, du_a, dg_b, du_b), mlp_rows, mlp_rows2, 0)
    d_h2_far = sum_far(d_h2_part, "y")
    d_h2_pass = sum_pass(d_h2_part, d_h2_far)
    d_h2_pass, h2 = together(d_h2_pass, h2)
    d_h2_near = sum_near(d_h2_pass, "y")
    mlp_grad = mlp_grads(h2, hid_a, dg_a, du_a, grads_b2)
    d_h2_near, mlp_grad = together(d_h2_near, mlp_grad)
    d_h2 = sum_of(d_h2_part, d_h2_near)
    d_middle = ct_own.astype(f32) + norm_back(d_h2, middle, inv_two, gains[1])
    da_own = d_middle.astype(bf16)
    da_near = gather_near(da_own, "y")
    out_part = back_through(slots, (hid_a, hid_b), mlp_rows, mlp_rows2, 2)
    da_near, out_part = together(da_near, out_part)
    da_far = gather_far(da_near, "y")
    da_pieces = (da_own, *da_near, *da_far)

    da, d_att = d_att_of(slots, da_pieces, w_attn, w_attn2)
    dq_far, d_kv2 = attend_back(slots, queries, kv2, far_places, d_att, attended, stats)
    d_kv2 = shift(d_kv2, "xh", 1)
    dq, d_kv = attend_back(
        slots, queries, kv, own_places, d_att, attended, stats, (dq_far,), (cos, sin)
    )
    dq, d_kv, d_kv2 = together(dq, d_kv, d_kv2)
    dkv_a, dkv_b, *d_h1_part = d_h1_of(slots, dq, d_kv, d_kv2, cos, sin, w_attn, w_attn2)
    d_h1_part, h1 = together(d_h1_part, h1)
    d_h1_far = sum_far(d_h1_part, "y")
    def attn_grads(h1, at, dkv, other=None):
        rights = [(0, dq, at, 256), (1, attended, at, 256), (0, dkv, 0, 128)]
        return weight_grads(slots, (h1, da), rights, other)

    grads_2 = attn_grads(h1, 256, dkv_b)
    d_h1_far, grads_2 = together(d_h1_far, grads_2)
    grads_2 = shift(grads_2, "c", 1)
    d_h1_near = sum_near(sum_pass(d_h1_part, d_h1_far), "y")
    grads_1 = attn_grads(h1, 0, dkv_a, grads_2)
    mlp_own = lax.psum_scatter(mlp_grad.reshape(2048, PARTS), TORUS, scatter_dimension=0, tiled=True)
    grads_1, d_h1_near = together(grads_1, d_h1_near)
    got = to_torus(grads_1.reshape(16, 128, 640))
    def to_y(grads):
        ring = [shift(grads[1], "y", -1), shift(grads[3], "y", 2), shift(grads[2], "y", 1), grads[0]]
        ring = jnp.stack(ring + ring[:3], 0)
        return lax.dynamic_slice_in_dim(ring, 3 - y, 4, 0).astype(f32)

    columns = lambda got: got.transpose(1, 0, 2).reshape(32, -1)
    grads = to_y(mlp_own.reshape(4, 32, PARTS))
    own_gate, own_up, own_down = (columns(grads[:, :, p * UNITS : p * UNITS + 704]) for p in range(3))
    d_h1 = sum_of(d_h1_part, d_h1_near)
    dx_own = (d_middle + norm_back(d_h1, x_own.astype(f32), inv_one[:128], gains[0])).astype(bf16)
    mlp_own, out_part = together(mlp_own, out_part)
    out_near = sum_near(sum_pass(out_part, sum_far(out_part, "y")), "y")
    out_own = (middle + sum_of(out_part, out_near)).astype(bf16)

    def both(a):
        other = shift(a, "c", 1)
        return jnp.where(core == 0, jnp.stack([a, other]), jnp.stack([other, a]))

    out, dx = both(out_own), both(dx_own)
    got, own_gate, own_up, own_down, out, dx = together(got, own_gate, own_up, own_down, out, dx)
    grads = to_y(got.astype(f32).sum(0).astype(bf16).reshape(4, 32, 640))
    own_q, own_o, own_kv = grads[:, :, :256], grads[:, :, 256:512], grads[:, :, 512:640]
    pair = lambda a: a.reshape(2, 2, 32, 64).sum(1).transpose(1, 0, 2).reshape(32, 128)
    own_q, own_o = columns(own_q), columns(own_o)
    own_k, own_v = pair(own_kv[:, :, :64]), pair(own_kv[:, :, 64:])

    def gain_grad(gain, *pairs):
        mine = sum(jnp.sum(w.astype(f32) * g, 1) for w, g in pairs)
        return (mine + shift(mine, "c", 1)) / gain.astype(f32)

    gain_two_grad = gain_grad(norm2_gain, (gate_weight, own_gate), (up_weight, own_up))
    gain_one_grad = gain_grad(norm1_gain, (q_weight, own_q), (k_weight, own_k), (v_weight, own_v))

    return (
        out,
        dx,
        gain_one_grad,
        own_q,
        own_k,
        own_v,
        own_o,
        gain_two_grad,
        own_gate,
        own_up,
        own_down,
    )


def solution(mesh):
    fine = Mesh(mesh.devices.reshape(4, 2, 4, 2, 2), ("z", "xl", "y", "xh", "c"))
    fsdp, cp = ("z", "xl"), ("y", "xh")
    acts, gain, weight = P(fsdp, cp, None), P(fsdp + cp), P(fsdp + cp, "c")
    return jax.shard_map(
        layer,
        mesh=fine,
        in_specs=(acts, P(fsdp, cp), acts, gain, weight, weight, weight, weight, gain, weight, weight, weight),
        out_specs=(acts, acts, gain, weight, weight, weight, weight, gain, weight, weight, weight),
        check_vma=False,
    )
```
